256 devices in a mesh: row: 16 (over x, y), col: 16 (over z, core).
Axes of the slice: x: 4, y: 4, z: 8, core: 2. Of those that a mesh axis runs over, the one named last changes fastest.
Arguments:
- basis: bfloat16 [64, 524288], P(None, ('col', 'row'))
- values: bfloat16 [2048, 2048, 128], P('row', 'col')
- block_row: int32 [16, 2048], P('row', 'col'), may hold values from 0 to 255
- block_col: int32 [16, 2048], P('row', 'col'), may hold values from 0 to 255
- block_count: int32 [16, 16], P('row', 'col'), may hold values from 1 to 128, as said below
Outputs:
- embedding: float32 [64, 524288], P(None, ('row', 'col'))
- factor: float32 [64, 64], replicated
The draws below stay inside these ranges and needn't reach their ends.
Inputs may be any that keep to these rules, and one draw needn't show every extreme that they name: `block_count`: every group stores at least one block, and at least one group fills all 128 slots.
All inputs are finite; a program needn't handle non-finite values.
Results may differ from the reference program's by a relative error of at most 0.0003.
Values may be sent and summed in bfloat16 or wider, within the bound.
No kernel may reach another device: no remote copies, remote signals or barrier semaphores. Data moves between devices by JAX's collectives and lax.ppermute only.
A program may use at most 64 MiB of HBM per device.

```python
import math
import jax
import jax.numpy as jnp
from jax import lax

K = 64
BS = 128
BLK_DEV = 16
NNZB_DEV = 128
NROWS = 524288
N_ROW = 16
N_COL = 16


def draw_basis(key, part):
    key = jax.random.fold_in(key, 11)
    first, second = jax.random.split(key, 2)
    field = jnp.clip(jax.random.normal(first, (K, NROWS), jnp.float32), -6.0, 6.0)
    column_scale = 10.0 ** jax.random.uniform(second, (K, 1), jnp.float32, 0.0, 1.0)
    return (field * column_scale).astype(jnp.bfloat16)


def draw_values(key, part):
    key = jax.random.fold_in(key, 7)
    shape = (N_ROW * NNZB_DEV, N_COL * BS, BS)
    fan_in = BS * NNZB_DEV // (2 * BLK_DEV)
    group = (jnp.arange(N_ROW * NNZB_DEV) // NNZB_DEV).astype(jnp.float32)
    rise = group / max(N_ROW - 1, 1)
    scale = (3.0 ** rise)[:, None, None]
    entries = jnp.clip(jax.random.normal(key, shape, jnp.float32), -6.0, 6.0)
    return (entries * scale * fan_in ** (-0.5)).astype(jnp.bfloat16)


def draw_block_count(key, part):
    key = jax.random.fold_in(key, 5)
    first, second, third = jax.random.split(key, 3)
    left = jax.random.randint(first, (N_ROW * N_COL,), 0, NNZB_DEV + 1)
    right = jax.random.randint(second, (N_ROW * N_COL,), 0, NNZB_DEV + 1)
    counts = jnp.maximum(1, NNZB_DEV - left * right // NNZB_DEV)
    chosen = jax.random.randint(third, (), 0, N_ROW * N_COL)
    counts = jnp.where(jnp.arange(N_ROW * N_COL) == chosen, NNZB_DEV, counts)
    return counts.reshape(N_ROW, N_COL).astype(jnp.int32)


def with_ends(array, rng, smallest, high):
    place = [jax.random.randint(jax.random.fold_in(rng, axis), (), 0, length) for axis, length in enumerate(array.shape)]
    main_axis = array.shape.index(max(array.shape))
    neighbour = place[:main_axis] + [(place[main_axis] + 1) % array.shape[main_axis]] + place[main_axis + 1:]
    return array.at[tuple(place)].set(smallest).at[tuple(neighbour)].set(high)


def setup_inputs(seed: int = 0) -> dict:
    seeds = jax.random.split(jax.random.key(seed), 6)
    return {
        "basis": draw_basis(jax.random.fold_in(seeds[5], 71), 0),
        "values": draw_values(jax.random.fold_in(seeds[5], 71), 0),
        "block_row": with_ends(jax.random.randint(seeds[2], (N_ROW, N_COL * NNZB_DEV), 0, BLK_DEV * N_COL), jax.random.fold_in(seeds[2], 1), 0, (BLK_DEV * N_COL) - 1).astype(jnp.int32),
        "block_col": with_ends(jax.random.randint(seeds[3], (N_ROW, N_COL * NNZB_DEV), 0, BLK_DEV * N_ROW), jax.random.fold_in(seeds[3], 1), 0, (BLK_DEV * N_ROW) - 1).astype(jnp.int32),
        "block_count": draw_block_count(jax.random.fold_in(seeds[5], 71), 0),
    }


def reference(basis, values, block_row, block_col, block_count):
    f32 = jnp.float32
    highest = lax.Precision.HIGHEST
    row_blocks = BLK_DEV * N_COL
    col_blocks = BLK_DEV * N_ROW
    slot = jnp.arange(NNZB_DEV, dtype=jnp.int32)
    targets = jnp.arange(row_blocks, dtype=jnp.int32)

    def per_row(r):
        vals_r = lax.dynamic_slice_in_dim(values, (r * NNZB_DEV).astype(jnp.int32), NNZB_DEV, 0)

        def per_col(acc, c):
            blocks = lax.dynamic_slice_in_dim(vals_r, (c * BS).astype(jnp.int32), BS, 1)
            rows = lax.dynamic_slice(block_row, (r.astype(jnp.int32), (c * NNZB_DEV).astype(jnp.int32)), (1, NNZB_DEV))[0]
            cols = lax.dynamic_slice(block_col, (r.astype(jnp.int32), (c * NNZB_DEV).astype(jnp.int32)), (1, NNZB_DEV))[0]
            count = block_count[r, c]
            slab = lax.dynamic_slice_in_dim(basis, (c * col_blocks * BS).astype(jnp.int32), col_blocks * BS, 1)
            picked = jnp.take(slab.reshape(K, col_blocks, BS), cols, axis=1)
            prods = jnp.einsum('ksj,sij->ski', picked.astype(f32), blocks.astype(f32), precision=highest)
            live = slot < count
            onehot = ((rows[None, :] == targets[:, None]) & live[None, :]).astype(f32)
            part = jnp.einsum('rs,ski->rki', onehot, prods, precision=highest)
            return (acc + part, None)
        acc, _ = lax.scan(per_col, jnp.zeros((row_blocks, K, BS), f32), jnp.arange(N_COL, dtype=jnp.int32))
        return acc
    slabs = lax.map(per_row, jnp.arange(N_ROW, dtype=jnp.int32))
    product = slabs.reshape(N_ROW * row_blocks, K, BS).transpose(1, 0, 2).reshape(K, NROWS)
    gram = jnp.dot(product, product.T, precision=highest)
    upper = jnp.linalg.cholesky(gram).T
    final = jax.scipy.linalg.solve_triangular(upper, product, trans=1, lower=False)
    scale = math.sqrt(NROWS)
    return (final * scale, upper / scale)
```

```python
import functools
import math

import jax
import jax.numpy as jnp
from jax import lax
from jax.experimental import pallas as pl
from jax.experimental.pallas import tpu as pltpu
from jax.sharding import PartitionSpec as P

GROUP = 8
HIGHEST = lax.Precision.HIGHEST


def product_kernel(rows, cols, count, slab, values, out):
    size = values.shape[1]
    per_part = slab.shape[2] // size
    out[...] = jnp.zeros_like(out)

    def block(slot):
        column = cols[0, slot]
        part = lax.div(column, per_part)
        offset = pl.multiple_of(lax.rem(column, per_part) * size, size)
        return lax.dot_general(
            slab[part, :, pl.ds(offset, size)],
            values[slot],
            (((1,), (1,)), ((), ())),
            preferred_element_type=jnp.float32,
        )

    def group(step, carry):
        first = step * GROUP
        made = [block(first + i) for i in range(GROUP)]
        for i in range(GROUP):
            row = rows[0, first + i]
            out[row] = out[row] + made[i]
        return carry

    def single(slot, carry):
        row = rows[0, slot]
        out[row] = out[row] + block(slot)
        return carry

    live = jnp.minimum(count[0, 0], values.shape[0])
    whole = lax.div(live, GROUP)
    lax.fori_loop(0, whole, group, 0)
    lax.fori_loop(whole * GROUP, live, single, 0)


def block_product(rows, cols, count, slab, values, row_blocks):
    slots, size, _ = values.shape
    width_k = slab.shape[1]
    smem = pl.BlockSpec(memory_space=pltpu.SMEM)
    vmem = pl.BlockSpec(memory_space=pltpu.VMEM)
    return pl.pallas_call(
        product_kernel,
        out_shape=jax.ShapeDtypeStruct((row_blocks, width_k, size), jnp.float32),
        in_specs=[smem, smem, smem, vmem, vmem],
        out_specs=vmem,
        compiler_params=pltpu.CompilerParams(vmem_limit_bytes=40 * 2**20),
        cost_estimate=pl.CostEstimate(
            flops=2 * slots * size * size * width_k,
            bytes_accessed=slab.size * 2 + values.size * 2 + row_blocks * width_k * size * 4,
            transcendentals=0,
        ),
    )(rows, cols, count, slab, values)


def gram_kernel(mine, out):
    total = jnp.zeros(out.shape, jnp.float32)
    for b in range(mine.shape[0]):
        total += lax.dot_general(
            mine[b], mine[b], (((1,), (1,)), ((), ())),
            precision=HIGHEST, preferred_element_type=jnp.float32,
        )
    out[...] = total


def local_gram(mine):
    width_k = mine.shape[1]
    return pl.pallas_call(
        gram_kernel,
        out_shape=jax.ShapeDtypeStruct((width_k, width_k), jnp.float32),
    )(mine)


def finish_kernel(scale, gram, mine, embedding, factor, work):
    order = gram.shape[0]
    tile = 8
    tiles = order // tile
    lane = lax.broadcasted_iota(jnp.int32, (tile, 2 * order), 1)
    sub = lax.broadcasted_iota(jnp.int32, (tile, 2 * order), 0)
    work[:, :order] = gram[...]
    work[:, order:] = jnp.zeros((order, order), jnp.float32)
    rest = []
    for t in range(tiles):
        here = work[t * tile : (t + 1) * tile, :]
        rest.append(jnp.where(lane == sub + (order + t * tile), 1.0, here))
    for j in range(order):
        t, s = divmod(j, tile)
        row = rest[t][s : s + 1, :]
        pivot = rest[t][s : s + 1, j : j + 1]
        root = lax.rsqrt(pivot)
        root = root * (1.5 - 0.5 * (pivot * root) * root)
        unit = row * root
        work[j : j + 1, :] = unit
        for u in range(t, tiles):
            rest[u] = rest[u] - (rest[u][:, j : j + 1] * root) * unit
    done = work[...]
    row_id = lax.broadcasted_iota(jnp.int32, (order, 2 * order), 0)
    lane_id = lax.broadcasted_iota(jnp.int32, (order, 2 * order), 1)
    upper = jnp.where(lane_id >= row_id, done, 0.0)[:, :order]
    lower = jnp.where(lane_id <= row_id + order, done, 0.0)[:, order:]
    factor[...] = upper * (1.0 / scale)
    lower = lower * scale
    size = mine.shape[2]
    for b in range(mine.shape[0]):
        embedding[:, b * size : (b + 1) * size] = lax.dot_general(
            lower, mine[b], (((1,), (0,)), ((), ())),
            precision=HIGHEST, preferred_element_type=jnp.float32,
        )


def finish(gram, mine, scale):
    blocks, width_k, size = mine.shape
    return pl.pallas_call(
        functools.partial(finish_kernel, scale),
        out_shape=(
            jax.ShapeDtypeStruct((width_k, blocks * size), jnp.float32),
            jax.ShapeDtypeStruct((width_k, width_k), jnp.float32),
        ),
        scratch_shapes=[pltpu.VMEM((width_k, 2 * width_k), jnp.float32)],
    )(gram, mine)


def add_over(value, axis):
    count = lax.axis_size(axis)
    step = 1
    while step < count:
        value = value + lax.ppermute(value, axis, [(i, i ^ step) for i in range(count)])
        step *= 2
    return value


def body(basis, values, block_row, block_col, block_count):
    width_k, width = basis.shape
    size = values.shape[2]
    row_blocks = width // size * lax.axis_size("col")
    total_rows = width * lax.axis_size("row") * lax.axis_size("col")
    slab = lax.all_gather(basis, "row")
    share = block_product(block_row, block_col, block_count, slab, values, row_blocks)
    mine = lax.psum_scatter(share, "col", scatter_dimension=0, tiled=True)
    gram = add_over(add_over(local_gram(mine), "col"), "row")
    return finish(gram, mine, math.sqrt(total_rows))


def solution(mesh):
    in_specs = (
        P(None, ("col", "row")),
        P("row", "col", None),
        P("row", "col"),
        P("row", "col"),
        P("row", "col"),
    )
    out_specs = (P(None, ("row", "col")), P())
    return jax.shard_map(body, mesh=mesh, in_specs=in_specs, out_specs=out_specs, check_vma=False)
```

```python
import functools
import math

import jax
import jax.numpy as jnp
from jax import lax
from jax.experimental import pallas as pl
from jax.experimental.pallas import tpu as pltpu
from jax.sharding import PartitionSpec as P

GROUP = 8
FINE = 16.0
PANEL = 4
HIGHEST = lax.Precision.HIGHEST


def listed(packed, side, want, entries, filler):
    slots = packed.shape[1]

    def place(step, filled):
        for i in range(GROUP):
            entry = packed[side, step * GROUP + i]
            entries[side, filled] = entry
            filled = filled + jnp.where((entry & 3) == want, 1, 0)
        return filled

    filled = lax.fori_loop(0, slots // GROUP, place, 0)
    for i in range(GROUP):
        entries[side, filled + i] = filler
    return filled


def add_products(entries, side, count, block, out):
    def make(step):
        return [block(step * GROUP + i) for i in range(GROUP)]

    def flush(step, made):
        for i in range(GROUP):
            row = (entries[side, step * GROUP + i] >> 10) & 511
            out[row] = out[row] + made[i]

    def loop(step, made):
        later = make(step)
        flush(step - 1, made)
        return later

    steps = jnp.maximum(lax.div(count + (GROUP - 1), GROUP), 1)
    flush(steps - 1, lax.fori_loop(1, steps, loop, make(0)))


def product(slab, side, entry, part_index, value):
    size = value.shape[0]
    part = part_index((entry >> 6) & 15)
    offset = pl.multiple_of(((entry >> 2) & 15) * size, size)
    return lax.dot_general(
        slab[part, side, :, pl.ds(offset, size)], value, (((1,), (1,)), ((), ())), preferred_element_type=jnp.float32
    )


def early_kernel(filler, packed, a0, b0, a1, b1, a3, b3, own_values, other_values, out, slab, blocks, entries, sems):
    copies = [
        pltpu.make_async_copy(values, blocks.at[n, pl.ds(0, values.shape[0])], sems.at[6 + n])
        for n, values in enumerate((own_values, other_values))
    ] + [
        pltpu.make_async_copy(piece, slab.at[pl.ds(2 * n, 2)], sems.at[n])
        for n, piece in enumerate((a0, b0, a1, b1, a3, b3))
    ]
    for copy in copies:
        copy.start()
    out[...] = jnp.zeros_like(out)
    counts = [listed(packed, side, 0, entries, filler) for side in range(2)]
    for copy in copies:
        copy.wait()
    for side in range(2):

        def block(n, side=side):
            entry = entries[side, n]
            return product(
                slab, side, entry, lambda part: jnp.where(part >= 12, part - 4, part), blocks[side, entry >> 19]
            )

        add_products(entries, side, counts[side], block, out)


def late_kernel(filler, packed, a2, b2, own_values, other_values, share, out, slab, blocks, entries, sems):
    copies = [
        pltpu.make_async_copy(piece, slab.at[pl.ds(2 * n, 2)], sems.at[n]) for n, piece in enumerate((a2, b2))
    ]
    for copy in copies:
        copy.start()
    counts = [listed(packed, side, 1, entries, filler | (2 << 8)) for side in range(2)]

    def fetch(side, n):
        source = (own_values, other_values)[side]
        return pltpu.make_async_copy(source.at[entries[side, n] >> 19], blocks.at[side, n], sems.at[2 + side])

    for side in range(2):
        lax.fori_loop(0, counts[side], lambda n, c, side=side: (fetch(side, n).start(), c)[1], 0)
    out[...] = share[...]
    for copy in copies:
        copy.wait()
    for side in range(2):
        lax.fori_loop(0, counts[side], lambda n, c, side=side: (fetch(side, n).wait(), c)[1], 0)
    for side in range(2):

        def block(n, side=side):
            return product(slab, side, entries[side, n], lambda part: part - 8, blocks[side, n])

        add_products(entries, side, counts[side], block, out)


def add_blocks(kernel, packed, pieces, own_values, other_values, before, row_blocks):
    slots, size, _ = own_values.shape
    half = pieces[0].shape[2]
    hbm = pl.BlockSpec(memory_space=pltpu.HBM)
    vmem = pl.BlockSpec(memory_space=pltpu.VMEM)
    return pl.pallas_call(
        functools.partial(kernel, row_blocks << 10),
        out_shape=jax.ShapeDtypeStruct((row_blocks + 1, half, size), jnp.float32),
        in_specs=[pl.BlockSpec(memory_space=pltpu.SMEM)]
        + [pl.BlockSpec(memory_space=pl.ANY)] * len(pieces)
        + [hbm] * 2
        + [vmem] * len(before),
        out_specs=vmem,
        scratch_shapes=[
            pltpu.VMEM((2 * len(pieces),) + pieces[0].shape[1:], jnp.bfloat16),
            pltpu.VMEM((2, slots + GROUP, size, size), jnp.bfloat16),
            pltpu.SMEM((2, slots + GROUP), jnp.int32),
            pltpu.SemaphoreType.DMA((len(pieces) + 2,)),
        ],
        compiler_params=pltpu.CompilerParams(vmem_limit_bytes=26 * 2**20),
        cost_estimate=pl.CostEstimate(
            flops=4 * slots * size * size * half, bytes_accessed=16 * 2**20, transcendentals=0
        ),
    )(packed, *pieces, own_values, other_values, *before)


def code_into(total, out):
    count = total.shape[0]
    top = jnp.abs(total[0])
    for b in range(1, count):
        top = jnp.maximum(top, jnp.abs(total[b]))
    top = jnp.maximum(top, 1e-30)
    power = jnp.ceil(FINE * (jnp.log2(top) - math.log2(32000.0)))
    out[count] = power.astype(jnp.int32).astype(jnp.int16)
    step = jnp.exp2(power * (-1.0 / FINE))
    for b in range(count):
        out[b] = jnp.round(total[b] * step).astype(jnp.int32).astype(jnp.int16)


def decoded(coded, b, step):
    return coded[b].astype(jnp.int32).astype(jnp.float32) * step


def step_of(coded):
    last = coded.shape[0] - 1
    return jnp.exp2(coded[last].astype(jnp.int32).astype(jnp.float32) * (1.0 / FINE))


def first_kernel(place, index, share, out_right, out_left):
    half = out_right.shape[0] - 1
    here = index[place]
    code_into(share.at[pl.ds(here, half)], out_right)
    code_into(share.at[pl.ds(here + half, half)], out_left)


def pass_kernel(place, begin, index, share, coded, out, total):
    count = coded.shape[0] - 1
    here = index[place]
    step = step_of(coded)
    for b in range(total.shape[0]):
        if begin <= b < begin + count:
            total[b] = share[here + b] + decoded(coded, b - begin, step)
        else:
            total[b] = share[here + b]
    code_into(total, out)


def last_kernel(place, index, share, right, left, out):
    here = index[place]
    step_right, step_left = step_of(right), step_of(left)
    for b in range(out.shape[0]):
        out[b] = share[here + b] + decoded(right, b, step_right) + decoded(left, b, step_left)


def on_chunk(kernel, index, share, coded, out_shape, scratch=()):
    vmem = pl.BlockSpec(memory_space=pltpu.VMEM)
    return pl.pallas_call(
        kernel,
        out_shape=out_shape,
        in_specs=[pl.BlockSpec(memory_space=pltpu.SMEM)] + [vmem] * (1 + len(coded)),
        out_specs=[vmem] * len(out_shape),
        scratch_shapes=list(scratch),
        compiler_params=pltpu.CompilerParams(vmem_limit_bytes=8 * 2**20),
        cost_estimate=pl.CostEstimate(flops=2**20, bytes_accessed=2**20, transcendentals=0),
    )(index, share, *coded)


def gram_kernel(core, ours, theirs, mine, out):
    count, half, _ = ours.shape
    first = core[0] == 0
    blocks = []
    for b in range(count):
        low = jnp.where(first, ours[b], theirs[b])
        high = jnp.where(first, theirs[b], ours[b])
        blocks.append(jnp.concatenate([low, high], axis=0))
    for b in range(count // 2):
        mine[b] = jnp.where(first, blocks[b], blocks[b + count // 2])
    wide = jnp.concatenate(blocks, axis=1)
    gram = lax.dot_general(
        wide, wide, (((1,), (1,)), ((), ())), precision=HIGHEST, preferred_element_type=jnp.float32
    )
    out[:, : 2 * half] = gram[:half]
    out[:, 2 * half :] = gram[half:]


def local_gram(core, ours, theirs):
    count, half, size = ours.shape
    vmem = pl.BlockSpec(memory_space=pltpu.VMEM)
    return pl.pallas_call(
        gram_kernel,
        out_shape=(
            jax.ShapeDtypeStruct((count // 2, 2 * half, size), jnp.float32),
            jax.ShapeDtypeStruct((half, 4 * half), jnp.float32),
        ),
        in_specs=[pl.BlockSpec(memory_space=pltpu.SMEM), vmem, vmem],
        out_specs=(vmem, vmem),
        compiler_params=pltpu.CompilerParams(vmem_limit_bytes=8 * 2**20),
    )(core, ours, theirs)


def finish_kernel(scale, grams, mine, embedding, factor, work):
    order = factor.shape[0]
    tile = 8
    tiles = order // tile
    total = grams[0]
    for n in range(1, grams.shape[0]):
        total = total + grams[n]
    work[: order // 2, :order] = total[:, :order]
    work[order // 2 :, :order] = total[:, order:]
    work[:, order:] = jnp.zeros((order, order), jnp.float32)
    lane = lax.broadcasted_iota(jnp.int32, (tile, 2 * order), 1)
    sub = lax.broadcasted_iota(jnp.int32, (tile, 2 * order), 0)
    rest = []
    for t in range(tiles):
        here = work[t * tile : (t + 1) * tile, :]
        rest.append(jnp.where(lane == sub + (order + t * tile), 1.0, here))
    shape = (tile, 2 * order)
    for j in range(0, order, PANEL):
        t, s = divmod(j, tile)
        rows = [rest[t][s + p : s + p + 1, :] for p in range(PANEL)]
        columns = [
            {u: jnp.broadcast_to(rest[u][:, j + p : j + p + 1], shape) for u in range(t, tiles)} for p in range(PANEL)
        ]
        for p in range(PANEL):
            pivot = columns[p][t][s + p : s + p + 1, :]
            root = lax.rsqrt(pivot)
            root = root * (1.5 - 0.5 * (pivot * root) * root)
            rows[p] = rows[p] * root
            work[j + p : j + p + 1, :] = rows[p]
            scaled = {u: columns[p][u] * root for u in range(t, tiles)}
            for q in range(p + 1, PANEL):
                across = scaled[t][s + q : s + q + 1, :]
                rows[q] = rows[q] - across * rows[p]
                for u in range(t, tiles):
                    columns[q][u] = columns[q][u] - scaled[u] * across
            for u in range(t, tiles):
                rest[u] = rest[u] - scaled[u] * rows[p]
    done = work[...]
    row_id = lax.broadcasted_iota(jnp.int32, (order, 2 * order), 0)
    lane_id = lax.broadcasted_iota(jnp.int32, (order, 2 * order), 1)
    upper = jnp.where(lane_id >= row_id, done, 0.0)[:, :order]
    lower = jnp.where(lane_id <= row_id + order, done, 0.0)[:, order:]
    factor[...] = upper * (1.0 / scale)
    wide = jnp.concatenate([mine[b] for b in range(mine.shape[0])], axis=1)
    embedding[...] = lax.dot_general(
        lower * scale, wide, (((1,), (0,)), ((), ())), precision=HIGHEST, preferred_element_type=jnp.float32
    )


def finish(grams, mine, scale):
    blocks, width_k, size = mine.shape
    vmem = pl.BlockSpec(memory_space=pltpu.VMEM)
    return pl.pallas_call(
        functools.partial(finish_kernel, scale),
        out_shape=(
            jax.ShapeDtypeStruct((width_k, blocks * size), jnp.float32),
            jax.ShapeDtypeStruct((width_k, width_k), jnp.float32),
        ),
        in_specs=[vmem, vmem],
        out_specs=(vmem, vmem),
        scratch_shapes=[pltpu.VMEM((width_k, 2 * width_k), jnp.float32)],
        compiler_params=pltpu.CompilerParams(vmem_limit_bytes=8 * 2**20),
    )(grams, mine)


SIDE = 4
BOTH = ("row", "col")


def permutes(rows, cols):
    depth = cols // 2

    def pairs(move):
        made = []
        for x in range(SIDE):
            for y in range(rows // SIDE):
                for z in range(depth):
                    for core in range(2):
                        a, b, c, d = move(x, y, z, core)
                        to = (a % SIDE) * (rows // SIDE) + b % (rows // SIDE)
                        made.append(
                            ((x * (rows // SIDE) + y) * cols + 2 * z + core, to * cols + 2 * (c % depth) + d)
                        )
        return made

    def along(first):
        def send(d):
            return pairs(lambda x, y, z, core: (x + d, y, z, core) if (core == 0) == first else (x, y + d, z, core))
        return send

    return (
        pairs(lambda x, y, z, core: (x, y, z, 1 - core)),
        along(True),
        along(False),
        lambda d: pairs(lambda x, y, z, core: (x, y, z + d, core)),
    )


def body(basis, values, block_row, block_col, block_count):
    width_k, width = basis.shape
    slots, size, _ = values.shape
    rows, cols = lax.axis_size("row"), lax.axis_size("col")
    half = width_k // 2
    per_device = width // size
    row_blocks = per_device * cols
    total_rows = width * rows * cols
    swap, first, second, deep = permutes(rows, cols)

    def move(array, pairs):
        return lax.ppermute(array, BOTH, pairs)

    row, col = lax.axis_index("row"), lax.axis_index("col")
    x, y = lax.div(row, SIDE), lax.rem(row, SIDE)
    z, core = lax.div(col, 2), lax.rem(col, 2)

    other_basis = move(basis, swap)
    values, other_basis = lax.optimization_barrier((values, other_basis))
    other_values = move(values, swap)

    def packed_for(which):
        slot = lax.broadcasted_iota(jnp.int32, block_row.shape, 1)
        source, offset = block_col >> 4, block_col & 15
        dx, dy = ((source >> 2) - x) & 3, (source - y) & 3
        near, far = jnp.where(which == 0, dx, dy), jnp.where(which == 0, dy, dx)
        key = jnp.where(slot < block_count, jnp.where(far == 2, 1, 0), 2)
        return key | (offset << 2) | (near << 6) | (far << 8) | (block_row << 10) | (slot << 19)

    packed = jnp.concatenate([packed_for(core), move(packed_for(1 - core), swap)])

    chunk = lax.dynamic_slice_in_dim(jnp.stack([basis, other_basis]), core * half, half, 1)
    from_low, from_high = move(chunk, first(1)), move(chunk, first(-1))
    a0 = jnp.stack([chunk, from_high])
    across = jnp.stack([move(from_low[0], first(1)), move(from_high[1], first(-1))])
    a3, a1 = move(a0, second(1)), move(a0, second(-1))
    b0 = jnp.stack([across, from_low])
    b1, b3 = move(b0, second(-1)), move(b0, second(1))
    a2, b2 = move(a3, second(1)), move(b1, second(-1))

    share = add_blocks(early_kernel, packed, (a0, b0, a1, b1, a3, b3), values, other_values, (), row_blocks)
    share = add_blocks(late_kernel, packed, (a2, b2), values, other_values, (share,), row_blocks)

    depth = cols // 2
    coded = jax.ShapeDtypeStruct((2 * per_device + 1, half, size), jnp.int16)
    part = jax.ShapeDtypeStruct((per_device + 1, half, size), jnp.int16)
    scratch = [pltpu.VMEM((2 * per_device, half, size), jnp.float32)]
    index = ((z + jnp.arange(depth, dtype=jnp.int32)) & (depth - 1)) * (2 * per_device)

    def run(kernel, d, arrays, shapes, scratch=()):
        return on_chunk(functools.partial(kernel, d % depth), index, share, arrays, shapes, scratch)

    right, left = run(first_kernel, depth // 2, [], [part, part])
    for d in range(depth // 2 - 1, 0, -1):
        right, left = move(right, deep(1)), move(left, deep(-1))
        begin = per_device if d == depth // 2 - 1 else 0
        (right,) = run(lambda place, *refs: pass_kernel(place, 0, *refs), d, [right], [coded], scratch)
        (left,) = run(lambda place, *refs, begin=begin: pass_kernel(place, begin, *refs), -d, [left], [coded], scratch)
    right, left = move(right, deep(1)), move(left, deep(-1))
    whole = jax.ShapeDtypeStruct((2 * per_device, half, size), jnp.float32)
    (ours,) = run(last_kernel, 0, [right, left], [whole])
    mine, gram = local_gram(core[None].astype(jnp.int32), ours, move(ours, swap))

    def spread(array, axis, groups):
        count = len(groups[0])
        copies = jnp.broadcast_to(array[None], (count,) + array.shape)
        return lax.all_to_all(copies, axis, 0, 0, axis_index_groups=groups)

    gram = spread(gram, "col", [list(range(c, cols, 2)) for c in range(2)]).sum(0)
    grams = spread(gram, "row", [list(range(rows))])
    return finish(grams, mine, math.sqrt(total_rows))


def solution(mesh):
    in_specs = (
        P(None, ("col", "row")),
        P("row", "col", None),
        P("row", "col"),
        P("row", "col"),
        P("row", "col"),
    )
    out_specs = (P(None, ("row", "col")), P())
    return jax.shard_map(body, mesh=mesh, in_specs=in_specs, out_specs=out_specs, check_vma=False)
```

```python
import functools
import math

import jax
import jax.numpy as jnp
from jax import lax
from jax.experimental import pallas as pl
from jax.experimental.pallas import tpu as pltpu
from jax.sharding import PartitionSpec as P

FINE = 16.0
PANEL = 4
VMEM_ASK = 20 * 2**20
HIGHEST = lax.Precision.HIGHEST


def add_products(group, lists, side, begin, count, filler, block, out):
    def entry(n):
        return jnp.where(n < count, lists[side, begin + n], filler)

    def make(step):
        made = []
        for i in range(0, group, 2):
            made += block(entry(step * group + i), entry(step * group + i + 1))
        return made

    def flush(step, made):
        for i in range(group):
            row = (entry(step * group + i) >> 10) & 511
            out[row] = out[row] + made[i]

    def loop(step, made):
        later = make(step)
        flush(step - 1, made)
        return later

    steps = jnp.maximum(lax.div(count + (group - 1), group), 1)
    flush(steps - 1, lax.fori_loop(1, steps, loop, make(0)))


def products(slab, side, entries, values):
    size = values[0].shape[0]
    left = []
    for entry in entries:
        offset = pl.multiple_of(((entry >> 2) & 15) * size, size)
        left.append(slab[(entry >> 6) & 15, side, :, pl.ds(offset, size)])
    both = lax.dot_general(
        jnp.concatenate(left, axis=0),
        jnp.concatenate(values, axis=0),
        (((1,), (1,)), ((), ())),
        preferred_element_type=jnp.float32,
    )
    half = left[0].shape[0]
    return [both[:half, :size], both[half:, size:]]


def load(pieces, slab, sems):
    copies, at = [], 0
    for n, piece in enumerate(pieces):
        copies.append(pltpu.make_async_copy(piece, slab.at[pl.ds(at, piece.shape[0])], sems.at[n]))
        at += piece.shape[0]
    for copy in copies:
        copy.start()
    return copies


def add_stage(stage, group, filler, lists, slab, blocks, out):
    slots = blocks.shape[1]
    for side in range(2):

        def block(*entries, side=side):
            return products(slab, side, entries, [blocks[side, entry >> 19] for entry in entries])

        begin, count = lists[side, slots + stage], lists[side, slots + 4 + stage]
        add_products(group, lists, side, begin, count, filler, block, out)


def early_kernel(filler, lists, a0, b0, b1, a3, own_values, other_values, out, blocks, slab, sems):
    copies = [
        pltpu.make_async_copy(values, blocks.at[n], sems.at[4 + n]) for n, values in enumerate((own_values, other_values))
    ]
    for copy in copies:
        copy.start()
    copies += load((a0, b0, b1, a3), slab, sems)
    out[...] = jnp.zeros_like(out)
    for copy in copies:
        copy.wait()
    add_stage(0, 32, filler, lists, slab, blocks, out)


def middle_kernel(filler, lists, a1, b3, blocks, share, out, slab, sems):
    copies = load((a1, b3), slab, sems)
    out[...] = share[...]
    for copy in copies:
        copy.wait()
    add_stage(1, 16, filler, lists, slab, blocks, out)


def late_kernel(filler, lists, a2, b2, index, blocks, share, out, out_right, out_left, slab, sems):
    copies = load((a2, b2), slab, sems)
    out[...] = share[...]
    for copy in copies:
        copy.wait()
    add_stage(2, 16, filler, lists, slab, blocks, out)
    half = out_right.shape[0] - 1
    far = index[4]
    code_into(out.at[pl.ds(far, half)], out_right)
    code_into(out.at[pl.ds(far + half, half)], out_left)


def add_blocks(kernel, flops, lists, pieces, values, whole, out_shape, row_blocks):
    smem = pl.BlockSpec(memory_space=pltpu.SMEM)
    vmem = pl.BlockSpec(memory_space=pltpu.VMEM)
    there = sum(piece.shape[0] for piece in pieces)
    pieces = tuple(pieces) + tuple(values)
    return pl.pallas_call(
        functools.partial(kernel, row_blocks << 10),
        out_shape=out_shape,
        in_specs=[smem]
        + [pl.BlockSpec(memory_space=pl.ANY)] * len(pieces)
        + [smem if array.ndim == 1 else vmem for array in whole],
        out_specs=[vmem] * len(out_shape),
        scratch_shapes=[
            pltpu.VMEM((there,) + pieces[0].shape[1:], jnp.bfloat16),
            pltpu.SemaphoreType.DMA((len(pieces),)),
        ],
        compiler_params=pltpu.CompilerParams(vmem_limit_bytes=VMEM_ASK),
        cost_estimate=pl.CostEstimate(flops=flops, bytes_accessed=12 * 2**20, transcendentals=0),
    )(lists, *pieces, *whole)


def code_into(total, out):
    count = total.shape[0]
    top = jnp.abs(total[0])
    for b in range(1, count):
        top = jnp.maximum(top, jnp.abs(total[b]))
    top = jnp.maximum(top, 1e-30)
    power = jnp.ceil(FINE * (jnp.log2(top) - math.log2(32000.0)))
    out[count] = power.astype(jnp.int32).astype(jnp.int16)
    step = jnp.exp2(power * (-1.0 / FINE))
    for b in range(count):
        out[b] = jnp.round(total[b] * step).astype(jnp.int32).astype(jnp.int16)


def decoded(coded, b, step):
    return coded[b].astype(jnp.int32).astype(jnp.float32) * step


def step_of(coded):
    last = coded.shape[0] - 1
    return jnp.exp2(coded[last].astype(jnp.int32).astype(jnp.float32) * (1.0 / FINE))


def pass_kernel(place, begin, index, share, coded, out, total):
    count = coded.shape[0] - 1
    here = index[place]
    step = step_of(coded)
    for b in range(total.shape[0]):
        if begin <= b < begin + count:
            total[b] = share[here + b] + decoded(coded, b - begin, step)
        else:
            total[b] = share[here + b]
    code_into(total, out)


def last_kernel(place, index, share, right, left, out):
    here = index[place]
    step_right, step_left = step_of(right), step_of(left)
    for b in range(out.shape[0]):
        out[b] = share[here + b] + decoded(right, b, step_right) + decoded(left, b, step_left)


def on_chunk(kernel, index, share, coded, out_shape, scratch=()):
    vmem = pl.BlockSpec(memory_space=pltpu.VMEM)
    return pl.pallas_call(
        kernel,
        out_shape=out_shape,
        in_specs=[pl.BlockSpec(memory_space=pltpu.SMEM)] + [vmem] * (1 + len(coded)),
        out_specs=[vmem] * len(out_shape),
        scratch_shapes=list(scratch),
        compiler_params=pltpu.CompilerParams(vmem_limit_bytes=8 * 2**20),
        cost_estimate=pl.CostEstimate(flops=2**20, bytes_accessed=2**20, transcendentals=0),
    )(index, share, *coded)


def gram_kernel(core, ours, theirs, mine, out):
    count, half, _ = ours.shape
    first = core[0] == 0
    blocks = []
    for b in range(count):
        low = jnp.where(first, ours[b], theirs[b])
        high = jnp.where(first, theirs[b], ours[b])
        blocks.append(jnp.concatenate([low, high], axis=0))
    for b in range(count // 2):
        mine[b] = jnp.where(first, blocks[b], blocks[b + count // 2])
    wide = jnp.concatenate(blocks, axis=1)
    gram = lax.dot_general(
        wide, wide, (((1,), (1,)), ((), ())), precision=HIGHEST, preferred_element_type=jnp.float32
    )
    out[:, : 2 * half] = gram[:half]
    out[:, 2 * half :] = gram[half:]


def local_gram(core, ours, theirs):
    count, half, size = ours.shape
    vmem = pl.BlockSpec(memory_space=pltpu.VMEM)
    return pl.pallas_call(
        gram_kernel,
        out_shape=(
            jax.ShapeDtypeStruct((count // 2, 2 * half, size), jnp.float32),
            jax.ShapeDtypeStruct((half, 4 * half), jnp.float32),
        ),
        in_specs=[pl.BlockSpec(memory_space=pltpu.SMEM), vmem, vmem],
        out_specs=(vmem, vmem),
        compiler_params=pltpu.CompilerParams(vmem_limit_bytes=8 * 2**20),
    )(core, ours, theirs)


def finish_kernel(scale, grams, mine, embedding, factor, work):
    order = factor.shape[0]
    tile = 8
    tiles = order // tile
    total = grams[0]
    for n in range(1, grams.shape[0]):
        total = total + grams[n]
    work[: order // 2, :order] = total[:, :order]
    work[order // 2 :, :order] = total[:, order:]
    work[:, order:] = jnp.zeros((order, order), jnp.float32)
    lane = lax.broadcasted_iota(jnp.int32, (tile, 2 * order), 1)
    sub = lax.broadcasted_iota(jnp.int32, (tile, 2 * order), 0)
    rest = []
    for t in range(tiles):
        here = work[t * tile : (t + 1) * tile, :]
        rest.append(jnp.where(lane == sub + (order + t * tile), 1.0, here))
    shape = (tile, 2 * order)
    for j in range(0, order, PANEL):
        t, s = divmod(j, tile)
        rows = [rest[t][s + p : s + p + 1, :] for p in range(PANEL)]
        columns = [
            {u: jnp.broadcast_to(rest[u][:, j + p : j + p + 1], shape) for u in range(t, tiles)} for p in range(PANEL)
        ]
        for p in range(PANEL):
            pivot = columns[p][t][s + p : s + p + 1, :]
            root = lax.rsqrt(pivot)
            root = root * (1.5 - 0.5 * (pivot * root) * root)
            rows[p] = rows[p] * root
            work[j + p : j + p + 1, :] = rows[p]
            scaled = {u: columns[p][u] * root for u in range(t, tiles)}
            for q in range(p + 1, PANEL):
                across = scaled[t][s + q : s + q + 1, :]
                rows[q] = rows[q] - across * rows[p]
                for u in range(t, tiles):
                    columns[q][u] = columns[q][u] - scaled[u] * across
            for u in range(t, tiles):
                rest[u] = rest[u] - scaled[u] * rows[p]
    done = work[...]
    row_id = lax.broadcasted_iota(jnp.int32, (order, 2 * order), 0)
    lane_id = lax.broadcasted_iota(jnp.int32, (order, 2 * order), 1)
    upper = jnp.where(lane_id >= row_id, done, 0.0)[:, :order]
    lower = jnp.where(lane_id <= row_id + order, done, 0.0)[:, order:]
    factor[...] = upper * (1.0 / scale)
    wide = jnp.concatenate([mine[b] for b in range(mine.shape[0])], axis=1)
    embedding[...] = lax.dot_general(
        lower * scale, wide, (((1,), (0,)), ((), ())), precision=HIGHEST, preferred_element_type=jnp.float32
    )


def finish(grams, mine, scale):
    blocks, width_k, size = mine.shape
    vmem = pl.BlockSpec(memory_space=pltpu.VMEM)
    return pl.pallas_call(
        functools.partial(finish_kernel, scale),
        out_shape=(
            jax.ShapeDtypeStruct((width_k, blocks * size), jnp.float32),
            jax.ShapeDtypeStruct((width_k, width_k), jnp.float32),
        ),
        in_specs=[vmem, vmem],
        out_specs=(vmem, vmem),
        scratch_shapes=[pltpu.VMEM((width_k, 2 * width_k), jnp.float32)],
        compiler_params=pltpu.CompilerParams(vmem_limit_bytes=8 * 2**20),
    )(grams, mine)


SIDE = 4
BOTH = ("row", "col")


def permutes(rows, cols):
    depth = cols // 2

    def pairs(move):
        made = []
        for x in range(SIDE):
            for y in range(rows // SIDE):
                for z in range(depth):
                    for core in range(2):
                        a, b, c, d = move(x, y, z, core)
                        to = (a % SIDE) * (rows // SIDE) + b % (rows // SIDE)
                        made.append(
                            ((x * (rows // SIDE) + y) * cols + 2 * z + core, to * cols + 2 * (c % depth) + d)
                        )
        return made

    def along(first):
        def send(d):
            return pairs(lambda x, y, z, core: (x + d, y, z, core) if (core == 0) == first else (x, y + d, z, core))
        return send

    return (
        pairs(lambda x, y, z, core: (x, y, z, 1 - core)),
        along(True),
        along(False),
        lambda d: pairs(lambda x, y, z, core: (x, y, z + d, core)),
    )


def body(basis, values, block_row, block_col, block_count):
    width_k, width = basis.shape
    slots, size, _ = values.shape
    rows, cols = lax.axis_size("row"), lax.axis_size("col")
    half = width_k // 2
    per_device = width // size
    row_blocks = per_device * cols
    total_rows = width * rows * cols
    swap, first, second, deep = permutes(rows, cols)

    def move(array, pairs):
        return lax.ppermute(array, BOTH, pairs)

    row, col = lax.axis_index("row"), lax.axis_index("col")
    x, y = lax.div(row, SIDE), lax.rem(row, SIDE)
    z, core = lax.div(col, 2), lax.rem(col, 2)

    other_basis = move(basis, swap)
    values, other_basis = lax.optimization_barrier((values, other_basis))
    other_values = move(values, swap)

    low, high = slice(0, half), slice(half, None)
    chunk = jnp.stack([jnp.where(core == 0, array[low], array[high]) for array in (basis, other_basis)])
    chunk, block_row, block_col, block_count = lax.optimization_barrier((chunk, block_row, block_col, block_count))

    def packed_for(which):
        slot = lax.broadcasted_iota(jnp.int32, block_row.shape, 1)
        source, offset = block_col >> 4, block_col & 15
        dx, dy = ((source >> 2) - x) & 3, (source - y) & 3
        near, far = jnp.where(which == 0, dx, dy), jnp.where(which == 0, dy, dx)
        middle = ((far == 1) & (near < 2)) | ((far == 3) & (near >= 2))
        stage = jnp.where(far == 2, 2, jnp.where(middle, 1, 0))
        place = near + jnp.where(stage > 0, 0, jnp.where(far == 0, 0, jnp.where(far == 1, 2, 6)))
        stage = jnp.where(slot < block_count, stage, 3)
        return stage | (offset << 2) | (place << 6) | (block_row << 10) | (slot << 19)

    def listed(packed):
        key = packed[0] & 3
        place = jnp.arange(slots, dtype=jnp.int32)
        order = key * slots + place
        rank = jnp.sum((order[:, None] < order[None, :]).astype(jnp.int32), axis=0)
        entries = jnp.sum(jnp.where(rank[None, :] == place[:, None], packed, 0), axis=1)
        begins = jnp.sum((key[None, :] < place[:4, None]).astype(jnp.int32), axis=1)
        counts = jnp.sum((key[None, :] == place[: slots - 4, None]).astype(jnp.int32), axis=1)
        return jnp.concatenate([entries, begins, counts])[None]

    other_lists = move(listed(packed_for(1 - core)), swap)
    from_low, from_high = move(chunk, first(1)), move(chunk, first(-1))
    depth = cols // 2
    index = ((z + jnp.arange(depth, dtype=jnp.int32)) & (depth - 1)) * (2 * per_device)
    which = core[None].astype(jnp.int32)
    from_low, from_high, other_lists, index, which = lax.optimization_barrier(
        (from_low, from_high, other_lists, index, which)
    )
    lists = jnp.concatenate([listed(packed_for(core)), other_lists])
    a0 = jnp.stack([chunk, from_high])
    across = jnp.stack([move(from_low[0], first(1)), move(from_high[1], first(-1))])
    a3, a1 = move(a0, second(1)), move(a0, second(-1))
    b0 = jnp.stack([across, from_low])
    b1, b3 = move(b0, second(-1)), move(b0, second(1))
    a2, b2 = move(a3, second(1)), move(b1, second(-1))

    coded = jax.ShapeDtypeStruct((2 * per_device + 1, half, size), jnp.int16)
    part = jax.ShapeDtypeStruct((per_device + 1, half, size), jnp.int16)
    scratch = [pltpu.VMEM((2 * per_device, half, size), jnp.float32)]

    total = jax.ShapeDtypeStruct((row_blocks + 1, half, size), jnp.float32)
    blocks = jax.ShapeDtypeStruct((2,) + values.shape, jnp.bfloat16)
    work = 4 * slots * size * size * half
    share, blocks = add_blocks(
        early_kernel, work // 2, lists, (a0, b0, b1, a3), (values, other_values), (), (total, blocks), row_blocks
    )
    (share,) = add_blocks(middle_kernel, work // 4, lists, (a1, b3), (), (blocks, share), (total,), row_blocks)
    share, right, left = add_blocks(
        late_kernel, work // 4, lists, (a2, b2), (), (index, blocks, share), (total, part, part), row_blocks
    )

    def run(kernel, d, arrays, shapes, scratch=()):
        return on_chunk(functools.partial(kernel, d % depth), index, share, arrays, shapes, scratch)

    for d in range(depth // 2 - 1, 0, -1):
        right, left = move(right, deep(1)), move(left, deep(-1))
        begin = per_device if d == depth // 2 - 1 else 0
        (right,) = run(lambda place, *refs: pass_kernel(place, 0, *refs), d, [right], [coded], scratch)
        (left,) = run(lambda place, *refs, begin=begin: pass_kernel(place, begin, *refs), -d, [left], [coded], scratch)
    right, left = move(right, deep(1)), move(left, deep(-1))
    whole = jax.ShapeDtypeStruct((2 * per_device, half, size), jnp.float32)
    (ours,) = run(last_kernel, 0, [right, left], [whole])
    mine, gram = local_gram(which, ours, move(ours, swap))

    def spread(array, axis, groups):
        count = len(groups[0])
        copies = jnp.broadcast_to(array[None], (count,) + array.shape)
        return lax.all_to_all(copies, axis, 0, 0, axis_index_groups=groups)

    gram = spread(gram, "col", [list(range(c, cols, 2)) for c in range(2)]).sum(0)
    grams = spread(gram, "row", [list(range(rows))])
    return finish(grams, mine, math.sqrt(total_rows))


def solution(mesh):
    in_specs = (
        P(None, ("col", "row")),
        P("row", "col", None),
        P("row", "col"),
        P("row", "col"),
        P("row", "col"),
    )
    out_specs = (P(None, ("row", "col")), P())
    return jax.shard_map(body, mesh=mesh, in_specs=in_specs, out_specs=out_specs, check_vma=False)
```

```python
import functools
import math

import jax
import jax.numpy as jnp
from jax import lax
from jax.experimental import pallas as pl
from jax.experimental.pallas import tpu as pltpu
from jax.sharding import PartitionSpec as P

FINE = 16.0
PANEL = 8
VMEM_ASK = 20 * 2**20
HIGHEST = lax.Precision.HIGHEST


def add_products(group, lists, side, begin, count, filler, block, out):
    def entry(n):
        return jnp.where(n < count, lists[side, begin + n], filler)

    def make(step):
        made = []
        for i in range(0, group, 2):
            made += block(entry(step * group + i), entry(step * group + i + 1))
        return made

    def flush(step, made):
        for i in range(group):
            row = (entry(step * group + i) >> 10) & 511
            out[row] = out[row] + made[i]

    def loop(step, made):
        later = make(step)
        flush(step - 1, made)
        return later

    steps = jnp.maximum(lax.div(count + (group - 1), group), 1)
    flush(steps - 1, lax.fori_loop(1, steps, loop, make(0)))


def products(slab, side, entries, values):
    size = values[0].shape[0]
    left = []
    for entry in entries:
        offset = pl.multiple_of(((entry >> 2) & 15) * size, size)
        left.append(slab[(entry >> 6) & 15, side, :, pl.ds(offset, size)])
    both = lax.dot_general(
        jnp.concatenate(left, axis=0),
        jnp.concatenate(values, axis=0),
        (((1,), (1,)), ((), ())),
        preferred_element_type=jnp.float32,
    )
    half = left[0].shape[0]
    return [both[:half, :size], both[half:, size:]]


def load(pieces, slab, sems):
    copies, at = [], 0
    for n, piece in enumerate(pieces):
        copies.append(pltpu.make_async_copy(piece, slab.at[pl.ds(at, piece.shape[0])], sems.at[n]))
        at += piece.shape[0]
    for copy in copies:
        copy.start()
    return copies


def add_stage(stage, group, filler, lists, slab, blocks, out):
    slots = blocks.shape[1]
    for side in range(2):

        def block(*entries, side=side):
            return products(slab, side, entries, [blocks[side, entry >> 19] for entry in entries])

        begin, count = lists[side, slots + stage], lists[side, slots + 4 + stage]
        add_products(group, lists, side, begin, count, filler, block, out)


def early_kernel(filler, lists, a0, b0, b1, a3, own_values, other_values, out, blocks, slab, sems):
    copies = [
        pltpu.make_async_copy(values, blocks.at[n], sems.at[4 + n]) for n, values in enumerate((own_values, other_values))
    ]
    for copy in copies:
        copy.start()
    copies += load((a0, b0, b1, a3), slab, sems)
    out[...] = jnp.zeros_like(out)
    for copy in copies:
        copy.wait()
    add_stage(0, 32, filler, lists, slab, blocks, out)


def middle_kernel(filler, lists, a1, b3, blocks, share, out, slab, sems):
    copies = load((a1, b3), slab, sems)
    out[...] = share[...]
    for copy in copies:
        copy.wait()
    add_stage(1, 16, filler, lists, slab, blocks, out)


def late_kernel(filler, lists, a2, b2, index, blocks, share, out, out_right, out_left, home, slab, sems):
    copies = load((a2, b2), slab, sems)
    out[...] = share[...]
    for copy in copies:
        copy.wait()
    add_stage(2, 16, filler, lists, slab, blocks, out)
    half = out_right.shape[0] - 1
    far = index[4]
    code_into(out.at[pl.ds(far, half)], out_right)
    code_into(out.at[pl.ds(far + half, half)], out_left)
    home[...] = out[pl.ds(index[0], home.shape[0])]


def add_blocks(kernel, flops, lists, pieces, values, whole, out_shape, row_blocks):
    smem = pl.BlockSpec(memory_space=pltpu.SMEM)
    vmem = pl.BlockSpec(memory_space=pltpu.VMEM)
    there = sum(piece.shape[0] for piece in pieces)
    pieces = tuple(pieces) + tuple(values)
    return pl.pallas_call(
        functools.partial(kernel, row_blocks << 10),
        out_shape=out_shape,
        in_specs=[smem]
        + [pl.BlockSpec(memory_space=pl.ANY)] * len(pieces)
        + [smem if array.ndim == 1 else vmem for array in whole],
        out_specs=[vmem] * len(out_shape),
        scratch_shapes=[
            pltpu.VMEM((there,) + pieces[0].shape[1:], jnp.bfloat16),
            pltpu.SemaphoreType.DMA((len(pieces),)),
        ],
        compiler_params=pltpu.CompilerParams(vmem_limit_bytes=VMEM_ASK),
        cost_estimate=pl.CostEstimate(flops=flops, bytes_accessed=12 * 2**20, transcendentals=0),
    )(lists, *pieces, *whole)


def code_into(total, out):
    count = total.shape[0]
    top = jnp.abs(total[0])
    for b in range(1, count):
        top = jnp.maximum(top, jnp.abs(total[b]))
    top = jnp.maximum(top, 1e-30)
    power = jnp.ceil(FINE * (jnp.log2(top) - math.log2(32000.0)))
    out[count] = power.astype(jnp.int32).astype(jnp.int16)
    step = jnp.exp2(power * (-1.0 / FINE))
    for b in range(count):
        out[b] = jnp.round(total[b] * step).astype(jnp.int32).astype(jnp.int16)


def decoded(coded, b, step):
    return coded[b].astype(jnp.int32).astype(jnp.float32) * step


def step_of(coded):
    last = coded.shape[0] - 1
    return jnp.exp2(coded[last].astype(jnp.int32).astype(jnp.float32) * (1.0 / FINE))


def pass_kernel(place, begin, index, share, coded, out, total):
    count = coded.shape[0] - 1
    here = index[place]
    step = step_of(coded)
    for b in range(total.shape[0]):
        if begin <= b < begin + count:
            total[b] = share[here + b] + decoded(coded, b - begin, step)
        else:
            total[b] = share[here + b]
    code_into(total, out)


def on_chunk(kernel, index, share, coded, out_shape, scratch=()):
    vmem = pl.BlockSpec(memory_space=pltpu.VMEM)
    return pl.pallas_call(
        kernel,
        out_shape=out_shape,
        in_specs=[pl.BlockSpec(memory_space=pltpu.SMEM)] + [vmem] * (1 + len(coded)),
        out_specs=[vmem] * len(out_shape),
        scratch_shapes=list(scratch),
        compiler_params=pltpu.CompilerParams(vmem_limit_bytes=8 * 2**20),
        cost_estimate=pl.CostEstimate(flops=2**20, bytes_accessed=2**20, transcendentals=0),
    )(index, share, *coded)


def gram_kernel(core, ours, right, left, theirs, their_right, their_left, mine, out):
    count, half, _ = ours.shape
    first = core[0] == 0
    parts = []
    for home, one, two in ((ours, right, left), (theirs, their_right, their_left)):
        step_one, step_two = step_of(one), step_of(two)
        parts.append([home[b] + decoded(one, b, step_one) + decoded(two, b, step_two) for b in range(count)])
    blocks = []
    for own, other in zip(*parts):
        blocks.append(jnp.concatenate([jnp.where(first, own, other), jnp.where(first, other, own)], axis=0))
    for b in range(count // 2):
        mine[b] = jnp.where(first, blocks[b], blocks[b + count // 2])
    wide = jnp.concatenate(blocks, axis=1)
    gram = lax.dot_general(
        wide, wide, (((1,), (1,)), ((), ())), precision=HIGHEST, preferred_element_type=jnp.float32
    )
    out[:, : 2 * half] = gram[:half]
    out[:, 2 * half :] = gram[half:]


def local_gram(core, *sums):
    count, half, size = sums[0].shape
    vmem = pl.BlockSpec(memory_space=pltpu.VMEM)
    return pl.pallas_call(
        gram_kernel,
        out_shape=(
            jax.ShapeDtypeStruct((count // 2, 2 * half, size), jnp.float32),
            jax.ShapeDtypeStruct((half, 4 * half), jnp.float32),
        ),
        in_specs=[pl.BlockSpec(memory_space=pltpu.SMEM)] + [vmem] * 6,
        out_specs=(vmem, vmem),
        compiler_params=pltpu.CompilerParams(vmem_limit_bytes=10 * 2**20),
        cost_estimate=pl.CostEstimate(flops=2**27, bytes_accessed=2**21, transcendentals=0),
    )(core, *sums)


def finish_kernel(scale, grams, mine, embedding, factor, work):
    order = factor.shape[0]
    tile = 8
    tiles = order // tile
    total = grams[0]
    for n in range(1, grams.shape[0]):
        total = total + grams[n]
    work[: order // 2, :order] = total[:, :order]
    work[order // 2 :, :order] = total[:, order:]
    work[:, order:] = jnp.zeros((order, order), jnp.float32)
    lane = lax.broadcasted_iota(jnp.int32, (tile, 2 * order), 1)
    sub = lax.broadcasted_iota(jnp.int32, (tile, 2 * order), 0)
    rest = []
    for t in range(tiles):
        here = work[t * tile : (t + 1) * tile, :]
        rest.append(jnp.where(lane == sub + (order + t * tile), 1.0, here))
    shape = (tile, 2 * order)
    for j in range(0, order, PANEL):
        t, s = divmod(j, tile)
        rows = [rest[t][s + p : s + p + 1, :] for p in range(PANEL)]
        columns = [
            {u: jnp.broadcast_to(rest[u][:, j + p : j + p + 1], shape) for u in range(t, tiles)} for p in range(PANEL)
        ]
        for p in range(PANEL):
            pivot = columns[p][t][s + p : s + p + 1, :]
            root = lax.rsqrt(pivot)
            rows[p] = rows[p] * root
            work[j + p : j + p + 1, :] = rows[p]
            scaled = {u: columns[p][u] * root for u in range(t, tiles)}
            for q in range(p + 1, PANEL):
                across = scaled[t][s + q : s + q + 1, :]
                rows[q] = rows[q] - across * rows[p]
                for u in range(t, tiles):
                    columns[q][u] = columns[q][u] - scaled[u] * across
            for u in range(t, tiles):
                rest[u] = rest[u] - scaled[u] * rows[p]
    done = work[...]
    row_id = lax.broadcasted_iota(jnp.int32, (order, 2 * order), 0)
    lane_id = lax.broadcasted_iota(jnp.int32, (order, 2 * order), 1)
    upper = jnp.where(lane_id >= row_id, done, 0.0)[:, :order]
    lower = jnp.where(lane_id <= row_id + order, done, 0.0)[:, order:]
    factor[...] = upper * (1.0 / scale)
    wide = jnp.concatenate([mine[b] for b in range(mine.shape[0])], axis=1)
    embedding[...] = lax.dot_general(
        lower * scale, wide, (((1,), (0,)), ((), ())), precision=HIGHEST, preferred_element_type=jnp.float32
    )


def finish(grams, mine, scale):
    blocks, width_k, size = mine.shape
    vmem = pl.BlockSpec(memory_space=pltpu.VMEM)
    return pl.pallas_call(
        functools.partial(finish_kernel, scale),
        out_shape=(
            jax.ShapeDtypeStruct((width_k, blocks * size), jnp.float32),
            jax.ShapeDtypeStruct((width_k, width_k), jnp.float32),
        ),
        in_specs=[vmem, vmem],
        out_specs=(vmem, vmem),
        scratch_shapes=[pltpu.VMEM((width_k, 2 * width_k), jnp.float32)],
        compiler_params=pltpu.CompilerParams(vmem_limit_bytes=8 * 2**20),
    )(grams, mine)


SIDE = 4
BOTH = ("row", "col")


def permutes(rows, cols):
    depth = cols // 2

    def pairs(move):
        made = []
        for x in range(SIDE):
            for y in range(rows // SIDE):
                for z in range(depth):
                    for core in range(2):
                        a, b, c, d = move(x, y, z, core)
                        to = (a % SIDE) * (rows // SIDE) + b % (rows // SIDE)
                        made.append(
                            ((x * (rows // SIDE) + y) * cols + 2 * z + core, to * cols + 2 * (c % depth) + d)
                        )
        return made

    def along(first):
        def send(d):
            return pairs(lambda x, y, z, core: (x + d, y, z, core) if (core == 0) == first else (x, y + d, z, core))
        return send

    return (
        pairs(lambda x, y, z, core: (x, y, z, 1 - core)),
        along(True),
        along(False),
        lambda d: pairs(lambda x, y, z, core: (x, y, z + d, core)),
    )


def body(basis, values, block_row, block_col, block_count):
    width_k, width = basis.shape
    slots, size, _ = values.shape
    rows, cols = lax.axis_size("row"), lax.axis_size("col")
    half = width_k // 2
    per_device = width // size
    row_blocks = per_device * cols
    total_rows = width * rows * cols
    swap, first, second, deep = permutes(rows, cols)

    def move(array, pairs):
        return lax.ppermute(array, BOTH, pairs)

    row, col = lax.axis_index("row"), lax.axis_index("col")
    x, y = lax.div(row, SIDE), lax.rem(row, SIDE)
    z, core = lax.div(col, 2), lax.rem(col, 2)

    other_basis = move(basis, swap)
    values, other_basis = lax.optimization_barrier((values, other_basis))
    other_values = move(values, swap)

    low, high = slice(0, half), slice(half, None)
    chunk = jnp.stack([jnp.where(core == 0, array[low], array[high]) for array in (basis, other_basis)])
    chunk, block_row, block_col, block_count = lax.optimization_barrier((chunk, block_row, block_col, block_count))

    def packed_for(which):
        slot = lax.broadcasted_iota(jnp.int32, block_row.shape, 1)
        source, offset = block_col >> 4, block_col & 15
        dx, dy = ((source >> 2) - x) & 3, (source - y) & 3
        near, far = jnp.where(which == 0, dx, dy), jnp.where(which == 0, dy, dx)
        middle = ((far == 1) & (near < 2)) | ((far == 3) & (near >= 2))
        stage = jnp.where(far == 2, 2, jnp.where(middle, 1, 0))
        place = near + jnp.where(stage > 0, 0, jnp.where(far == 0, 0, jnp.where(far == 1, 2, 6)))
        stage = jnp.where(slot < block_count, stage, 3)
        return stage | (offset << 2) | (place << 6) | (block_row << 10) | (slot << 19)

    def listed(packed):
        key = packed[0] & 3
        place = jnp.arange(slots, dtype=jnp.int32)
        order = key * slots + place
        rank = jnp.sum((order[:, None] < order[None, :]).astype(jnp.int32), axis=0)
        entries = jnp.sum(jnp.where(rank[None, :] == place[:, None], packed, 0), axis=1)
        begins = jnp.sum((key[None, :] < place[:4, None]).astype(jnp.int32), axis=1)
        counts = jnp.sum((key[None, :] == place[: slots - 4, None]).astype(jnp.int32), axis=1)
        return jnp.concatenate([entries, begins, counts])[None]

    other_lists = move(listed(packed_for(1 - core)), swap)
    from_low, from_high = move(chunk, first(1)), move(chunk, first(-1))
    far_own, far_other = move(chunk[0], first(2)), move(chunk[1], first(-2))
    depth = cols // 2
    index = ((z + jnp.arange(depth, dtype=jnp.int32)) & (depth - 1)) * (2 * per_device)
    which = core[None].astype(jnp.int32)
    from_low, from_high, other_lists, index, which = lax.optimization_barrier(
        (from_low, from_high, other_lists, index, which)
    )
    lists = jnp.concatenate([listed(packed_for(core)), other_lists])
    a0 = jnp.stack([chunk, from_high])
    across = jnp.stack([far_own, far_other])
    a3, a1 = move(a0, second(1)), move(a0, second(-1))
    b0 = jnp.stack([across, from_low])
    b1, b3 = move(b0, second(-1)), move(b0, second(1))
    a2, b2 = move(a3, second(1)), move(b1, second(-1))

    coded = jax.ShapeDtypeStruct((2 * per_device + 1, half, size), jnp.int16)
    part = jax.ShapeDtypeStruct((per_device + 1, half, size), jnp.int16)
    scratch = [pltpu.VMEM((2 * per_device, half, size), jnp.float32)]

    total = jax.ShapeDtypeStruct((row_blocks + 1, half, size), jnp.float32)
    blocks = jax.ShapeDtypeStruct((2,) + values.shape, jnp.bfloat16)
    work = 4 * slots * size * size * half
    share, blocks = add_blocks(
        early_kernel, work // 2, lists, (a0, b0, b1, a3), (values, other_values), (), (total, blocks), row_blocks
    )
    (share,) = add_blocks(middle_kernel, work // 4, lists, (a1, b3), (), (blocks, share), (total,), row_blocks)
    whole = jax.ShapeDtypeStruct((2 * per_device, half, size), jnp.float32)
    share, right, left, home = add_blocks(
        late_kernel, work // 4, lists, (a2, b2), (), (index, blocks, share), (total, part, part, whole), row_blocks
    )
    their_home = move(home, swap)

    def run(kernel, d, arrays, shapes, scratch=()):
        return on_chunk(functools.partial(kernel, d % depth), index, share, arrays, shapes, scratch)

    for d in range(depth // 2 - 1, 0, -1):
        right, left = move(right, deep(1)), move(left, deep(-1))
        begin = per_device if d == depth // 2 - 1 else 0
        (right,) = run(lambda place, *refs: pass_kernel(place, 0, *refs), d, [right], [coded], scratch)
        (left,) = run(lambda place, *refs, begin=begin: pass_kernel(place, begin, *refs), -d, [left], [coded], scratch)
    right, left = move(right, deep(1)), move(left, deep(-1))
    mine, gram = local_gram(which, home, right, left, their_home, move(right, swap), move(left, swap))

    def spread(array, axis, groups):
        count = len(groups[0])
        copies = jnp.broadcast_to(array[None], (count,) + array.shape)
        return lax.all_to_all(copies, axis, 0, 0, axis_index_groups=groups)

    gram = spread(gram, "col", [list(range(c, cols, 2)) for c in range(2)]).sum(0)
    grams = spread(gram, "row", [list(range(rows))])
    return finish(grams, mine, math.sqrt(total_rows))


def solution(mesh):
    in_specs = (
        P(None, ("col", "row")),
        P("row", "col", None),
        P("row", "col"),
        P("row", "col"),
        P("row", "col"),
    )
    out_specs = (P(None, ("row", "col")), P())
    return jax.shard_map(body, mesh=mesh, in_specs=in_specs, out_specs=out_specs, check_vma=False)
```

```python
import functools
import math

import jax
import jax.numpy as jnp
from jax import lax
from jax.experimental import pallas as pl
from jax.experimental.pallas import tpu as pltpu
from jax.sharding import PartitionSpec as P

FINE = 16.0
PANEL = 8
VMEM_ASK = 20 * 2**20
HIGHEST = lax.Precision.HIGHEST


def add_products(group, lists, side, begin, count, filler, block, out):
    def entry(n):
        return jnp.where(n < count, lists[side, begin + n], filler)

    def make(step):
        made = []
        for i in range(0, group, 2):
            made += block(entry(step * group + i), entry(step * group + i + 1))
        return made

    def flush(step, made):
        for i in range(group):
            row = (entry(step * group + i) >> 11) & 511
            out[row] = out[row] + made[i]

    def loop(step, made):
        later = make(step)
        flush(step - 1, made)
        return later

    steps = jnp.maximum(lax.div(count + (group - 1), group), 1)
    flush(steps - 1, lax.fori_loop(1, steps, loop, make(0)))


def products(slab, side, entries, values):
    size = values[0].shape[0]
    left = []
    for entry in entries:
        offset = pl.multiple_of(((entry >> 3) & 15) * size, size)
        left.append(slab[(entry >> 7) & 15, side, :, pl.ds(offset, size)])
    both = lax.dot_general(
        jnp.concatenate(left, axis=0),
        jnp.concatenate(values, axis=0),
        (((1,), (1,)), ((), ())),
        preferred_element_type=jnp.float32,
    )
    half = left[0].shape[0]
    return [both[:half, :size], both[half:, size:]]


def load(pieces, slab, sems):
    copies, at = [], 0
    for n, piece in enumerate(pieces):
        copies.append(pltpu.make_async_copy(piece, slab.at[pl.ds(at, piece.shape[0])], sems.at[n]))
        at += piece.shape[0]
    for copy in copies:
        copy.start()
    return copies


def add_stage(stage, group, filler, lists, slab, blocks, out):
    slots = blocks.shape[1]
    for side in range(2):

        def block(*entries, side=side):
            return products(slab, side, entries, [blocks[side, entry >> 20] for entry in entries])

        begin, count = lists[side, slots + stage], lists[side, slots + 8 + stage]
        add_products(group, lists, side, begin, count, filler, block, out)


def early_kernel(filler, lists, a0, b0, b1, a3, own_values, other_values, out, blocks, slab, sems):
    copies = [
        pltpu.make_async_copy(values, blocks.at[n], sems.at[4 + n]) for n, values in enumerate((own_values, other_values))
    ]
    for copy in copies:
        copy.start()
    copies += load((a0, b0, b1, a3), slab, sems)
    out[...] = jnp.zeros_like(out)
    for copy in copies:
        copy.wait()
    add_stage(0, 32, filler, lists, slab, blocks, out)


def middle_kernel(filler, lists, a1, b3, blocks, share, out, slab, sems):
    copies = load((a1, b3), slab, sems)
    out[...] = share[...]
    for copy in copies:
        copy.wait()
    add_stage(1, 16, filler, lists, slab, blocks, out)


def late_kernel(filler, lists, a2, b2, index, blocks, share, out, out_right, out_left, slab, sems):
    copies = load((a2, b2), slab, sems)
    out[...] = share[...]
    for copy in copies:
        copy.wait()
    add_stage(2, 4, filler, lists, slab, blocks, out)
    half = out_right.shape[0] - 1
    far = index[4]
    code_into(out.at[pl.ds(far, half)], out_right)
    code_into(out.at[pl.ds(far + half, half)], out_left)


def last_kernel(filler, lists, a2, b2, index, blocks, share, out, home, slab, sems):
    copies = load((a2, b2), slab, sems)
    out[...] = share[...]
    for copy in copies:
        copy.wait()
    add_stage(3, 16, filler, lists, slab, blocks, out)
    home[...] = out[pl.ds(index[0], home.shape[0])]


def add_blocks(kernel, flops, lists, pieces, values, whole, out_shape, row_blocks):
    smem = pl.BlockSpec(memory_space=pltpu.SMEM)
    vmem = pl.BlockSpec(memory_space=pltpu.VMEM)
    there = sum(piece.shape[0] for piece in pieces)
    pieces = tuple(pieces) + tuple(values)
    return pl.pallas_call(
        functools.partial(kernel, row_blocks << 11),
        out_shape=out_shape,
        in_specs=[smem]
        + [pl.BlockSpec(memory_space=pl.ANY)] * len(pieces)
        + [smem if array.ndim == 1 else vmem for array in whole],
        out_specs=[vmem] * len(out_shape),
        scratch_shapes=[
            pltpu.VMEM((there,) + pieces[0].shape[1:], jnp.bfloat16),
            pltpu.SemaphoreType.DMA((len(pieces),)),
        ],
        compiler_params=pltpu.CompilerParams(vmem_limit_bytes=VMEM_ASK),
        cost_estimate=pl.CostEstimate(flops=flops, bytes_accessed=12 * 2**20, transcendentals=0),
    )(lists, *pieces, *whole)


def code_into(total, out):
    count = total.shape[0]
    top = jnp.abs(total[0])
    for b in range(1, count):
        top = jnp.maximum(top, jnp.abs(total[b]))
    top = jnp.maximum(top, 1e-30)
    power = jnp.ceil(FINE * (jnp.log2(top) - math.log2(32000.0)))
    out[count] = power.astype(jnp.int32).astype(jnp.int16)
    step = jnp.exp2(power * (-1.0 / FINE))
    for b in range(count):
        out[b] = jnp.round(total[b] * step).astype(jnp.int32).astype(jnp.int16)


def decoded(coded, b, step):
    return coded[b].astype(jnp.int32).astype(jnp.float32) * step


def step_of(coded):
    last = coded.shape[0] - 1
    return jnp.exp2(coded[last].astype(jnp.int32).astype(jnp.float32) * (1.0 / FINE))


def pass_kernel(place, begin, index, share, coded, out, total):
    count = coded.shape[0] - 1
    here = index[place]
    step = step_of(coded)
    for b in range(total.shape[0]):
        if begin <= b < begin + count:
            total[b] = share[here + b] + decoded(coded, b - begin, step)
        else:
            total[b] = share[here + b]
    code_into(total, out)


def on_chunk(kernel, index, share, coded, out_shape, scratch=()):
    vmem = pl.BlockSpec(memory_space=pltpu.VMEM)
    return pl.pallas_call(
        kernel,
        out_shape=out_shape,
        in_specs=[pl.BlockSpec(memory_space=pltpu.SMEM)] + [vmem] * (1 + len(coded)),
        out_specs=[vmem] * len(out_shape),
        scratch_shapes=list(scratch),
        compiler_params=pltpu.CompilerParams(vmem_limit_bytes=8 * 2**20),
        cost_estimate=pl.CostEstimate(flops=2**20, bytes_accessed=2**20, transcendentals=0),
    )(index, share, *coded)


def gram_kernel(core, ours, right, left, theirs, their_right, their_left, mine, out):
    count, half, _ = ours.shape
    first = core[0] == 0
    parts = []
    for home, one, two in ((ours, right, left), (theirs, their_right, their_left)):
        step_one, step_two = step_of(one), step_of(two)
        parts.append([home[b] + decoded(one, b, step_one) + decoded(two, b, step_two) for b in range(count)])
    blocks = []
    for own, other in zip(*parts):
        blocks.append(jnp.concatenate([jnp.where(first, own, other), jnp.where(first, other, own)], axis=0))
    for b in range(count // 2):
        mine[b] = jnp.where(first, blocks[b], blocks[b + count // 2])
    wide = jnp.concatenate(blocks, axis=1)
    gram = lax.dot_general(
        wide, wide, (((1,), (1,)), ((), ())), precision=HIGHEST, preferred_element_type=jnp.float32
    )
    out[:, : 2 * half] = gram[:half]
    out[:, 2 * half :] = gram[half:]


def local_gram(core, *sums):
    count, half, size = sums[0].shape
    vmem = pl.BlockSpec(memory_space=pltpu.VMEM)
    return pl.pallas_call(
        gram_kernel,
        out_shape=(
            jax.ShapeDtypeStruct((count // 2, 2 * half, size), jnp.float32),
            jax.ShapeDtypeStruct((half, 4 * half), jnp.float32),
        ),
        in_specs=[pl.BlockSpec(memory_space=pltpu.SMEM)] + [vmem] * 6,
        out_specs=(vmem, vmem),
        compiler_params=pltpu.CompilerParams(vmem_limit_bytes=10 * 2**20),
        cost_estimate=pl.CostEstimate(flops=2**27, bytes_accessed=2**21, transcendentals=0),
    )(core, *sums)


def finish_kernel(scale, grams, mine, embedding, factor, work):
    order = factor.shape[0]
    tile = 8
    tiles = order // tile
    total = grams[0]
    for n in range(1, grams.shape[0]):
        total = total + grams[n]
    work[: order // 2, :order] = total[:, :order]
    work[order // 2 :, :order] = total[:, order:]
    work[:, order:] = jnp.zeros((order, order), jnp.float32)
    lane = lax.broadcasted_iota(jnp.int32, (tile, 2 * order), 1)
    sub = lax.broadcasted_iota(jnp.int32, (tile, 2 * order), 0)
    rest = []
    for t in range(tiles):
        here = work[t * tile : (t + 1) * tile, :]
        rest.append(jnp.where(lane == sub + (order + t * tile), 1.0, here))
    shape = (tile, 2 * order)
    for j in range(0, order, PANEL):
        t, s = divmod(j, tile)
        rows = [rest[t][s + p : s + p + 1, :] for p in range(PANEL)]
        columns = [
            {u: jnp.broadcast_to(rest[u][:, j + p : j + p + 1], shape) for u in range(t, tiles)} for p in range(PANEL)
        ]
        for p in range(PANEL):
            pivot = columns[p][t][s + p : s + p + 1, :]
            root = lax.rsqrt(pivot)
            rows[p] = rows[p] * root
            work[j + p : j + p + 1, :] = rows[p]
            scaled = {u: columns[p][u] * root for u in range(t, tiles)}
            for q in range(p + 1, PANEL):
                across = scaled[t][s + q : s + q + 1, :]
                rows[q] = rows[q] - across * rows[p]
                for u in range(t, tiles):
                    columns[q][u] = columns[q][u] - scaled[u] * across
            for u in range(t, tiles):
                rest[u] = rest[u] - scaled[u] * rows[p]
    done = work[...]
    row_id = lax.broadcasted_iota(jnp.int32, (order, 2 * order), 0)
    lane_id = lax.broadcasted_iota(jnp.int32, (order, 2 * order), 1)
    upper = jnp.where(lane_id >= row_id, done, 0.0)[:, :order]
    lower = jnp.where(lane_id <= row_id + order, done, 0.0)[:, order:]
    factor[...] = upper * (1.0 / scale)
    wide = jnp.concatenate([mine[b] for b in range(mine.shape[0])], axis=1)
    embedding[...] = lax.dot_general(
        lower * scale, wide, (((1,), (0,)), ((), ())), precision=HIGHEST, preferred_element_type=jnp.float32
    )


def finish(grams, mine, scale):
    blocks, width_k, size = mine.shape
    vmem = pl.BlockSpec(memory_space=pltpu.VMEM)
    return pl.pallas_call(
        functools.partial(finish_kernel, scale),
        out_shape=(
            jax.ShapeDtypeStruct((width_k, blocks * size), jnp.float32),
            jax.ShapeDtypeStruct((width_k, width_k), jnp.float32),
        ),
        in_specs=[vmem, vmem],
        out_specs=(vmem, vmem),
        scratch_shapes=[pltpu.VMEM((width_k, 2 * width_k), jnp.float32)],
        compiler_params=pltpu.CompilerParams(vmem_limit_bytes=8 * 2**20),
    )(grams, mine)


SIDE = 4
BOTH = ("row", "col")


def permutes(rows, cols):
    depth = cols // 2

    def pairs(move):
        made = []
        for x in range(SIDE):
            for y in range(rows // SIDE):
                for z in range(depth):
                    for core in range(2):
                        a, b, c, d = move(x, y, z, core)
                        to = (a % SIDE) * (rows // SIDE) + b % (rows // SIDE)
                        made.append(
                            ((x * (rows // SIDE) + y) * cols + 2 * z + core, to * cols + 2 * (c % depth) + d)
                        )
        return made

    def along(first):
        def send(d):
            return pairs(lambda x, y, z, core: (x + d, y, z, core) if (core == 0) == first else (x, y + d, z, core))
        return send

    return (
        pairs(lambda x, y, z, core: (x, y, z, 1 - core)),
        along(True),
        along(False),
        lambda d: pairs(lambda x, y, z, core: (x, y, z + d, core)),
    )


def body(basis, values, block_row, block_col, block_count):
    width_k, width = basis.shape
    slots, size, _ = values.shape
    rows, cols = lax.axis_size("row"), lax.axis_size("col")
    half = width_k // 2
    per_device = width // size
    row_blocks = per_device * cols
    total_rows = width * rows * cols
    swap, first, second, deep = permutes(rows, cols)

    def move(array, pairs):
        return lax.ppermute(array, BOTH, pairs)

    row, col = lax.axis_index("row"), lax.axis_index("col")
    x, y = lax.div(row, SIDE), lax.rem(row, SIDE)
    z, core = lax.div(col, 2), lax.rem(col, 2)

    other_basis = move(basis, swap)
    values, other_basis = lax.optimization_barrier((values, other_basis))
    other_values = move(values, swap)

    depth = cols // 2
    low, high = slice(0, half), slice(half, None)
    chunk = jnp.stack([jnp.where(core == 0, array[low], array[high]) for array in (basis, other_basis)])
    chunk, block_row, block_col, block_count = lax.optimization_barrier((chunk, block_row, block_col, block_count))

    def packed_for(which):
        slot = lax.broadcasted_iota(jnp.int32, block_row.shape, 1)
        source, offset = block_col >> 4, block_col & 15
        dx, dy = ((source >> 2) - x) & 3, (source - y) & 3
        near, far = jnp.where(which == 0, dx, dy), jnp.where(which == 0, dy, dx)
        middle = ((far == 1) & (near < 2)) | ((far == 3) & (near >= 2))
        farthest = (lax.div(block_row, 2 * per_device) - z) & (depth - 1)
        stage = jnp.where(far == 2, jnp.where(farthest == depth // 2, 2, 3), jnp.where(middle, 1, 0))
        place = near + jnp.where(stage > 0, 0, jnp.where(far == 0, 0, jnp.where(far == 1, 2, 6)))
        stage = jnp.where(slot < block_count, stage, 4)
        return stage | (offset << 3) | (place << 7) | (block_row << 11) | (slot << 20)

    def listed(packed):
        key = packed[0] & 7
        place = jnp.arange(slots, dtype=jnp.int32)
        order = key * slots + place
        rank = jnp.sum((order[:, None] < order[None, :]).astype(jnp.int32), axis=0)
        entries = jnp.sum(jnp.where(rank[None, :] == place[:, None], packed, 0), axis=1)
        begins = jnp.sum((key[None, :] < place[:8, None]).astype(jnp.int32), axis=1)
        counts = jnp.sum((key[None, :] == place[: slots - 8, None]).astype(jnp.int32), axis=1)
        return jnp.concatenate([entries, begins, counts])[None]

    other_lists = move(listed(packed_for(1 - core)), swap)
    from_low, from_high = move(chunk, first(1)), move(chunk, first(-1))
    far_own, far_other = move(chunk[0], first(2)), move(chunk[1], first(-2))
    index = ((z + jnp.arange(depth, dtype=jnp.int32)) & (depth - 1)) * (2 * per_device)
    which = core[None].astype(jnp.int32)
    from_low, from_high, other_lists, index, which = lax.optimization_barrier(
        (from_low, from_high, other_lists, index, which)
    )
    lists = jnp.concatenate([listed(packed_for(core)), other_lists])
    a0 = jnp.stack([chunk, from_high])
    across = jnp.stack([far_own, far_other])
    a3, a1 = move(a0, second(1)), move(a0, second(-1))
    b0 = jnp.stack([across, from_low])
    b1, b3 = move(b0, second(-1)), move(b0, second(1))
    a2, b2 = move(a3, second(1)), move(b1, second(-1))

    coded = jax.ShapeDtypeStruct((2 * per_device + 1, half, size), jnp.int16)
    part = jax.ShapeDtypeStruct((per_device + 1, half, size), jnp.int16)
    scratch = [pltpu.VMEM((2 * per_device, half, size), jnp.float32)]

    total = jax.ShapeDtypeStruct((row_blocks + 1, half, size), jnp.float32)
    blocks = jax.ShapeDtypeStruct((2,) + values.shape, jnp.bfloat16)
    work = 4 * slots * size * size * half
    share, blocks = add_blocks(
        early_kernel, work // 2, lists, (a0, b0, b1, a3), (values, other_values), (), (total, blocks), row_blocks
    )
    (share,) = add_blocks(middle_kernel, work // 4, lists, (a1, b3), (), (blocks, share), (total,), row_blocks)
    whole = jax.ShapeDtypeStruct((2 * per_device, half, size), jnp.float32)
    share, right, left = add_blocks(
        late_kernel, work // 16, lists, (a2, b2), (), (index, blocks, share), (total, part, part), row_blocks
    )
    share, home = add_blocks(
        last_kernel, work // 4, lists, (a2, b2), (), (index, blocks, share), (total, whole), row_blocks
    )
    their_home = move(home, swap)

    def run(kernel, d, arrays, shapes, scratch=()):
        return on_chunk(functools.partial(kernel, d % depth), index, share, arrays, shapes, scratch)

    for d in range(depth // 2 - 1, 0, -1):
        right, left = move(right, deep(1)), move(left, deep(-1))
        begin = per_device if d == depth // 2 - 1 else 0
        (right,) = run(lambda place, *refs: pass_kernel(place, 0, *refs), d, [right], [coded], scratch)
        (left,) = run(lambda place, *refs, begin=begin: pass_kernel(place, begin, *refs), -d, [left], [coded], scratch)
    right, left = move(right, deep(1)), move(left, deep(-1))
    mine, gram = local_gram(which, home, right, left, their_home, move(right, swap), move(left, swap))

    def spread(array, axis, groups):
        count = len(groups[0])
        copies = jnp.broadcast_to(array[None], (count,) + array.shape)
        return lax.all_to_all(copies, axis, 0, 0, axis_index_groups=groups)

    gram = spread(gram, "col", [list(range(c, cols, 2)) for c in range(2)]).sum(0)
    grams = spread(gram, "row", [list(range(rows))])
    return finish(grams, mine, math.sqrt(total_rows))


def solution(mesh):
    in_specs = (
        P(None, ("col", "row")),
        P("row", "col", None),
        P("row", "col"),
        P("row", "col"),
        P("row", "col"),
    )
    out_specs = (P(None, ("row", "col")), P())
    return jax.shard_map(body, mesh=mesh, in_specs=in_specs, out_specs=out_specs, check_vma=False)
```

```python
import functools
import math

import jax
import jax.numpy as jnp
from jax import lax
from jax.experimental import pallas as pl
from jax.experimental.pallas import tpu as pltpu
from jax.sharding import PartitionSpec as P

FINE = 16.0
PANEL = 8
VMEM_ASK = 20 * 2**20
HIGHEST = lax.Precision.HIGHEST


def add_products(group, lists, side, begin, count, filler, block, out):
    def entry(n):
        return jnp.where(n < count, lists[side, begin + n], filler)

    def make(step):
        made = []
        for i in range(0, group, 2):
            made += block(entry(step * group + i), entry(step * group + i + 1))
        return made

    def flush(step, made):
        for i in range(group):
            row = (entry(step * group + i) >> 11) & 511
            out[row] = out[row] + made[i]

    def loop(step, made):
        later = make(step)
        flush(step - 1, made)
        return later

    steps = jnp.maximum(lax.div(count + (group - 1), group), 1)
    flush(steps - 1, lax.fori_loop(1, steps, loop, make(0)))


def products(slab, side, entries, values):
    size = values[0].shape[0]
    left = []
    for entry in entries:
        offset = pl.multiple_of(((entry >> 3) & 15) * size, size)
        left.append(slab[(entry >> 7) & 15, side, :, pl.ds(offset, size)])
    both = lax.dot_general(
        jnp.concatenate(left, axis=0),
        jnp.concatenate(values, axis=0),
        (((1,), (1,)), ((), ())),
        preferred_element_type=jnp.float32,
    )
    half = left[0].shape[0]
    return [both[:half, :size], both[half:, size:]]


def load(pieces, slab, sems):
    copies, at = [], 0
    for n, piece in enumerate(pieces):
        copies.append(pltpu.make_async_copy(piece, slab.at[pl.ds(at, piece.shape[0])], sems.at[n]))
        at += piece.shape[0]
    for copy in copies:
        copy.start()
    return copies


def add_stage(stage, group, filler, lists, slab, blocks, out):
    slots = blocks.shape[1]
    for side in range(2):

        def block(*entries, side=side):
            return products(slab, side, entries, [blocks[side, entry >> 20] for entry in entries])

        begin, count = lists[side, slots + stage], lists[side, slots + 8 + stage]
        add_products(group, lists, side, begin, count, filler, block, out)


def early_kernel(filler, lists, a0, b0, b1, a3, own_values, other_values, out, blocks, slab, sems):
    copies = [
        pltpu.make_async_copy(values, blocks.at[n], sems.at[4 + n]) for n, values in enumerate((own_values, other_values))
    ]
    for copy in copies:
        copy.start()
    copies += load((a0, b0, b1, a3), slab, sems)
    out[...] = jnp.zeros_like(out)
    for copy in copies:
        copy.wait()
    add_stage(0, 32, filler, lists, slab, blocks, out)


def middle_kernel(filler, lists, a1, b3, blocks, share, out, slab, sems):
    copies = load((a1, b3), slab, sems)
    out[...] = share[...]
    for copy in copies:
        copy.wait()
    add_stage(1, 16, filler, lists, slab, blocks, out)


def late_kernel(filler, lists, a2, b2, index, blocks, share, out, out_right, out_left, slab, sems):
    copies = load((a2, b2), slab, sems)
    out[...] = share[...]
    for copy in copies:
        copy.wait()
    add_stage(2, 4, filler, lists, slab, blocks, out)
    half = out_right.shape[0] - 1
    far = index[4]
    code_into(out.at[pl.ds(far, half)], out_right)
    code_into(out.at[pl.ds(far + half, half)], out_left)


def last_kernel(filler, lists, a2, b2, index, blocks, share, out, home, slab, sems):
    copies = load((a2, b2), slab, sems)
    out[...] = share[...]
    for copy in copies:
        copy.wait()
    add_stage(3, 16, filler, lists, slab, blocks, out)
    home[...] = out[pl.ds(index[0], home.shape[0])]


def add_blocks(kernel, flops, lists, pieces, values, whole, out_shape, row_blocks):
    smem = pl.BlockSpec(memory_space=pltpu.SMEM)
    vmem = pl.BlockSpec(memory_space=pltpu.VMEM)
    there = sum(piece.shape[0] for piece in pieces)
    pieces = tuple(pieces) + tuple(values)
    return pl.pallas_call(
        functools.partial(kernel, row_blocks << 11),
        out_shape=out_shape,
        in_specs=[smem]
        + [pl.BlockSpec(memory_space=pl.ANY)] * len(pieces)
        + [smem if array.ndim == 1 else vmem for array in whole],
        out_specs=[vmem] * len(out_shape),
        scratch_shapes=[
            pltpu.VMEM((there,) + pieces[0].shape[1:], jnp.bfloat16),
            pltpu.SemaphoreType.DMA((len(pieces),)),
        ],
        compiler_params=pltpu.CompilerParams(vmem_limit_bytes=VMEM_ASK),
        cost_estimate=pl.CostEstimate(flops=flops, bytes_accessed=12 * 2**20, transcendentals=0),
    )(lists, *pieces, *whole)


def code_into(total, out):
    count = total.shape[0]
    top = jnp.abs(total[0])
    for b in range(1, count):
        top = jnp.maximum(top, jnp.abs(total[b]))
    top = jnp.maximum(top, 1e-30)
    power = jnp.ceil(FINE * (jnp.log2(top) - math.log2(32000.0)))
    out[count] = power.astype(jnp.int32).astype(jnp.int16)
    step = jnp.exp2(power * (-1.0 / FINE))
    for b in range(count):
        out[b] = jnp.round(total[b] * step).astype(jnp.int32).astype(jnp.int16)


def decoded(coded, b, step):
    return coded[b].astype(jnp.int32).astype(jnp.float32) * step


def step_of(coded):
    last = coded.shape[0] - 1
    return jnp.exp2(coded[last].astype(jnp.int32).astype(jnp.float32) * (1.0 / FINE))


def pass_kernel(place, begin, index, share, coded, out, total):
    count = coded.shape[0] - 1
    here = index[place]
    step = step_of(coded)
    for b in range(total.shape[0]):
        if begin <= b < begin + count:
            total[b] = share[here + b] + decoded(coded, b - begin, step)
        else:
            total[b] = share[here + b]
    code_into(total, out)


def on_chunk(kernel, index, share, coded, out_shape, scratch=()):
    vmem = pl.BlockSpec(memory_space=pltpu.VMEM)
    return pl.pallas_call(
        kernel,
        out_shape=out_shape,
        in_specs=[pl.BlockSpec(memory_space=pltpu.SMEM)] + [vmem] * (1 + len(coded)),
        out_specs=[vmem] * len(out_shape),
        scratch_shapes=list(scratch),
        compiler_params=pltpu.CompilerParams(vmem_limit_bytes=8 * 2**20),
        cost_estimate=pl.CostEstimate(flops=2**20, bytes_accessed=2**20, transcendentals=0),
    )(index, share, *coded)


def gram_kernel(core, ours, right, left, theirs, their_right, their_left, mine, out):
    count, half, _ = ours.shape
    first = core[0] == 0
    parts = []
    for home, one, two in ((ours, right, left), (theirs, their_right, their_left)):
        step_one, step_two = step_of(one), step_of(two)
        parts.append([home[b] + decoded(one, b, step_one) + decoded(two, b, step_two) for b in range(count)])
    blocks = []
    for own, other in zip(*parts):
        blocks.append(jnp.concatenate([jnp.where(first, own, other), jnp.where(first, other, own)], axis=0))
    for b in range(count // 2):
        mine[b] = jnp.where(first, blocks[b], blocks[b + count // 2])
    wide = jnp.concatenate(blocks, axis=1)
    gram = lax.dot_general(
        wide, wide, (((1,), (1,)), ((), ())), precision=HIGHEST, preferred_element_type=jnp.float32
    )
    quarter, few = half // 2, half // 4
    out[:quarter, : 2 * half] = gram[:quarter]
    out[:quarter, 2 * half :] = gram[quarter:half]
    for n in range(4):
        out[quarter:, n * half : (n + 1) * half] = gram[half + n * few : half + (n + 1) * few, half:]


def local_gram(core, *sums):
    count, half, size = sums[0].shape
    vmem = pl.BlockSpec(memory_space=pltpu.VMEM)
    return pl.pallas_call(
        gram_kernel,
        out_shape=(
            jax.ShapeDtypeStruct((count // 2, 2 * half, size), jnp.float32),
            jax.ShapeDtypeStruct((half // 2 + half // 4, 4 * half), jnp.float32),
        ),
        in_specs=[pl.BlockSpec(memory_space=pltpu.SMEM)] + [vmem] * 6,
        out_specs=(vmem, vmem),
        compiler_params=pltpu.CompilerParams(vmem_limit_bytes=10 * 2**20),
        cost_estimate=pl.CostEstimate(flops=2**27, bytes_accessed=2**21, transcendentals=0),
    )(core, *sums)


def finish_kernel(scale, grams, mine, embedding, factor, work):
    order = factor.shape[0]
    tile = 8
    tiles = order // tile
    total = grams[0]
    for n in range(1, grams.shape[0]):
        total = total + grams[n]
    half, quarter, few = order // 2, order // 4, order // 8
    work[:quarter, :order] = total[:quarter, :order]
    work[quarter:half, :order] = total[:quarter, order:]
    for n in range(4):
        work[half + n * few : half + (n + 1) * few, half:order] = total[quarter:, n * half : (n + 1) * half]
    work[half:, :half] = work[:half, half:order].T
    work[:, order:] = jnp.zeros((order, order), jnp.float32)
    lane = lax.broadcasted_iota(jnp.int32, (tile, 2 * order), 1)
    sub = lax.broadcasted_iota(jnp.int32, (tile, 2 * order), 0)
    rest = []
    for t in range(tiles):
        here = work[t * tile : (t + 1) * tile, :]
        rest.append(jnp.where(lane == sub + (order + t * tile), 1.0, here))
    shape = (tile, 2 * order)
    for j in range(0, order, PANEL):
        t, s = divmod(j, tile)
        rows = [rest[t][s + p : s + p + 1, :] for p in range(PANEL)]
        columns = [
            {u: jnp.broadcast_to(rest[u][:, j + p : j + p + 1], shape) for u in range(t, tiles)} for p in range(PANEL)
        ]
        for p in range(PANEL):
            pivot = columns[p][t][s + p : s + p + 1, :]
            root = lax.rsqrt(pivot)
            rows[p] = rows[p] * root
            work[j + p : j + p + 1, :] = rows[p]
            scaled = {u: columns[p][u] * root for u in range(t, tiles)}
            for q in range(p + 1, PANEL):
                across = scaled[t][s + q : s + q + 1, :]
                rows[q] = rows[q] - across * rows[p]
                for u in range(t, tiles):
                    columns[q][u] = columns[q][u] - scaled[u] * across
            for u in range(t, tiles):
                rest[u] = rest[u] - scaled[u] * rows[p]
    done = work[...]
    row_id = lax.broadcasted_iota(jnp.int32, (order, 2 * order), 0)
    lane_id = lax.broadcasted_iota(jnp.int32, (order, 2 * order), 1)
    upper = jnp.where(lane_id >= row_id, done, 0.0)[:, :order]
    lower = jnp.where(lane_id <= row_id + order, done, 0.0)[:, order:]
    factor[...] = upper * (1.0 / scale)
    wide = jnp.concatenate([mine[b] for b in range(mine.shape[0])], axis=1)
    embedding[...] = lax.dot_general(
        lower * scale, wide, (((1,), (0,)), ((), ())), precision=HIGHEST, preferred_element_type=jnp.float32
    )


def finish(grams, mine, scale):
    blocks, width_k, size = mine.shape
    vmem = pl.BlockSpec(memory_space=pltpu.VMEM)
    return pl.pallas_call(
        functools.partial(finish_kernel, scale),
        out_shape=(
            jax.ShapeDtypeStruct((width_k, blocks * size), jnp.float32),
            jax.ShapeDtypeStruct((width_k, width_k), jnp.float32),
        ),
        in_specs=[vmem, vmem],
        out_specs=(vmem, vmem),
        scratch_shapes=[pltpu.VMEM((width_k, 2 * width_k), jnp.float32)],
        compiler_params=pltpu.CompilerParams(vmem_limit_bytes=8 * 2**20),
    )(grams, mine)


SIDE = 4
BOTH = ("row", "col")


def permutes(rows, cols):
    depth = cols // 2

    def pairs(move):
        made = []
        for x in range(SIDE):
            for y in range(rows // SIDE):
                for z in range(depth):
                    for core in range(2):
                        a, b, c, d = move(x, y, z, core)
                        to = (a % SIDE) * (rows // SIDE) + b % (rows // SIDE)
                        made.append(
                            ((x * (rows // SIDE) + y) * cols + 2 * z + core, to * cols + 2 * (c % depth) + d)
                        )
        return made

    def along(first):
        def send(d):
            return pairs(lambda x, y, z, core: (x + d, y, z, core) if (core == 0) == first else (x, y + d, z, core))
        return send

    return (
        pairs(lambda x, y, z, core: (x, y, z, 1 - core)),
        along(True),
        along(False),
        lambda d: pairs(lambda x, y, z, core: (x, y, z + d, core)),
    )


def body(basis, values, block_row, block_col, block_count):
    width_k, width = basis.shape
    slots, size, _ = values.shape
    rows, cols = lax.axis_size("row"), lax.axis_size("col")
    half = width_k // 2
    per_device = width // size
    row_blocks = per_device * cols
    total_rows = width * rows * cols
    swap, first, second, deep = permutes(rows, cols)

    def move(array, pairs):
        return lax.ppermute(array, BOTH, pairs)

    row, col = lax.axis_index("row"), lax.axis_index("col")
    x, y = lax.div(row, SIDE), lax.rem(row, SIDE)
    z, core = lax.div(col, 2), lax.rem(col, 2)

    other_basis = move(basis, swap)
    values, other_basis = lax.optimization_barrier((values, other_basis))
    other_values = move(values, swap)

    depth = cols // 2
    low, high = slice(0, half), slice(half, None)
    chunk = jnp.stack([jnp.where(core == 0, array[low], array[high]) for array in (basis, other_basis)])
    chunk, block_row, block_col, block_count = lax.optimization_barrier((chunk, block_row, block_col, block_count))

    def packed_for(which):
        slot = lax.broadcasted_iota(jnp.int32, block_row.shape, 1)
        source, offset = block_col >> 4, block_col & 15
        dx, dy = ((source >> 2) - x) & 3, (source - y) & 3
        near, far = jnp.where(which == 0, dx, dy), jnp.where(which == 0, dy, dx)
        middle = ((far == 1) & (near < 2)) | ((far == 3) & (near >= 2))
        farthest = (lax.div(block_row, 2 * per_device) - z) & (depth - 1)
        stage = jnp.where(far == 2, jnp.where(farthest == depth // 2, 2, 3), jnp.where(middle, 1, 0))
        place = near + jnp.where(stage > 0, 0, jnp.where(far == 0, 0, jnp.where(far == 1, 2, 6)))
        stage = jnp.where(slot < block_count, stage, 4)
        return stage | (offset << 3) | (place << 7) | (block_row << 11) | (slot << 20)

    def listed(packed):
        key = packed[0] & 7
        place = jnp.arange(slots, dtype=jnp.int32)
        order = key * slots + place
        rank = jnp.sum((order[:, None] < order[None, :]).astype(jnp.int32), axis=0)
        entries = jnp.sum(jnp.where(rank[None, :] == place[:, None], packed, 0), axis=1)
        begins = jnp.sum((key[None, :] < place[:8, None]).astype(jnp.int32), axis=1)
        counts = jnp.sum((key[None, :] == place[: slots - 8, None]).astype(jnp.int32), axis=1)
        return jnp.concatenate([entries, begins, counts])[None]

    other_lists = move(listed(packed_for(1 - core)), swap)
    from_low, from_high = move(chunk, first(1)), move(chunk, first(-1))
    far_own, far_other = move(chunk[0], first(2)), move(chunk[1], first(-2))
    index = ((z + jnp.arange(depth, dtype=jnp.int32)) & (depth - 1)) * (2 * per_device)
    which = core[None].astype(jnp.int32)
    from_low, from_high, other_lists, index, which = lax.optimization_barrier(
        (from_low, from_high, other_lists, index, which)
    )
    lists = jnp.concatenate([listed(packed_for(core)), other_lists])
    a0 = jnp.stack([chunk, from_high])
    across = jnp.stack([far_own, far_other])
    a3, a1 = move(a0, second(1)), move(a0, second(-1))
    b0 = jnp.stack([across, from_low])
    b1, b3 = move(b0, second(-1)), move(b0, second(1))
    a2, b2 = move(a3, second(1)), move(b1, second(-1))

    coded = jax.ShapeDtypeStruct((2 * per_device + 1, half, size), jnp.int16)
    part = jax.ShapeDtypeStruct((per_device + 1, half, size), jnp.int16)
    scratch = [pltpu.VMEM((2 * per_device, half, size), jnp.float32)]

    total = jax.ShapeDtypeStruct((row_blocks + 1, half, size), jnp.float32)
    blocks = jax.ShapeDtypeStruct((2,) + values.shape, jnp.bfloat16)
    work = 4 * slots * size * size * half
    share, blocks = add_blocks(
        early_kernel, work // 2, lists, (a0, b0, b1, a3), (values, other_values), (), (total, blocks), row_blocks
    )
    (share,) = add_blocks(middle_kernel, work // 4, lists, (a1, b3), (), (blocks, share), (total,), row_blocks)
    whole = jax.ShapeDtypeStruct((2 * per_device, half, size), jnp.float32)
    share, right, left = add_blocks(
        late_kernel, work // 16, lists, (a2, b2), (), (index, blocks, share), (total, part, part), row_blocks
    )
    share, home = add_blocks(
        last_kernel, work // 4, lists, (a2, b2), (), (index, blocks, share), (total, whole), row_blocks
    )
    their_home = move(home, swap)

    def run(kernel, d, arrays, shapes, scratch=()):
        return on_chunk(functools.partial(kernel, d % depth), index, share, arrays, shapes, scratch)

    for d in range(depth // 2 - 1, 0, -1):
        right, left = move(right, deep(1)), move(left, deep(-1))
        begin = per_device if d == depth // 2 - 1 else 0
        (right,) = run(lambda place, *refs: pass_kernel(place, 0, *refs), d, [right], [coded], scratch)
        (left,) = run(lambda place, *refs, begin=begin: pass_kernel(place, begin, *refs), -d, [left], [coded], scratch)
    right, left = move(right, deep(1)), move(left, deep(-1))
    mine, gram = local_gram(which, home, right, left, their_home, move(right, swap), move(left, swap))

    def spread(array, axis, groups):
        count = len(groups[0])
        copies = jnp.broadcast_to(array[None], (count,) + array.shape)
        return lax.all_to_all(copies, axis, 0, 0, axis_index_groups=groups)

    gram = spread(gram, "col", [list(range(c, cols, 2)) for c in range(2)]).sum(0)
    grams = spread(gram, "row", [list(range(rows))])
    return finish(grams, mine, math.sqrt(total_rows))


def solution(mesh):
    in_specs = (
        P(None, ("col", "row")),
        P("row", "col", None),
        P("row", "col"),
        P("row", "col"),
        P("row", "col"),
    )
    out_specs = (P(None, ("row", "col")), P())
    return jax.shard_map(body, mesh=mesh, in_specs=in_specs, out_specs=out_specs, check_vma=False)
```
